512 devices in a mesh: gx: 16 (over z), gy: 8 (over x_lo, y), gz: 4 (over x_hi, core).
Axes of the slice: x: 4 (x_hi: 2, x_lo: 2; x = x_hi * 2 + x_lo), y: 4, z: 16, core: 2. Of those that a mesh axis runs over, the one named last changes fastest.
Arguments:
- atom_x: float32 [16, 32, 256], P('gx', ('gy', 'gz')), may hold values from 0 to 23.99
- atom_y: float32 [16, 32, 256], P('gx', ('gy', 'gz')), may hold values from 0 to 11.99
- atom_z: float32 [16, 32, 256], P('gx', ('gy', 'gz')), may hold values from 0 to 384
- charges: float32 [16, 32, 256], P('gx', ('gy', 'gz')), may hold values from -4.5 to 4.5
- counts: int32 [16, 32], P('gx', ('gy', 'gz')), may hold values from 32 to 256, as said below
- background: float32 [384, 384, 384], P(('gy', 'gz'), 'gx'), may hold values from -0.3125 to 0.3125
Outputs:
- forces: float32 [3, 16, 32, 256], P(None, 'gx', ('gy', 'gz'))
The draws below stay inside these ranges and needn't reach their ends.
Inputs may be any that keep to these rules, and one draw needn't show every extreme that they name: `counts`: live slots come first in each pencil; some pencil is full in every draw.
All inputs are finite; a program needn't handle non-finite values.
Results may differ from the reference program's by a relative error of at most 0.0003.
Values sent between devices are 32-bit elements; how exact they have to be, the bound alone decides.
A program may use at most 128 MiB of HBM per device.

```python
import math
import jax
import jax.numpy as jnp
from jax import lax

NX = 384
NY = 384
NZ = 384
SLOTS = 256
PENCIL_X = 16
PENCIL_Y = 32


def draw_counts(key, part):
    key_list = jax.random.split(key, 4)
    extent = (PENCIL_X, PENCIL_Y)
    light_load = jax.random.randint(key_list[0], extent, max(SLOTS // 8, 1), SLOTS // 2 + 1)
    heavy_load = jax.random.randint(key_list[1], extent, SLOTS // 2, SLOTS + 1)
    selector = jax.random.randint(key_list[2], extent, 0, 8)
    loads = jnp.where(selector == 0, heavy_load, light_load).reshape(-1)
    full_pencil = jax.random.randint(key_list[3], (), 0, PENCIL_X * PENCIL_Y)
    loads = loads.at[full_pencil].set(SLOTS)
    return loads.reshape(PENCIL_X, PENCIL_Y).astype(jnp.int32)


def draw_charges(key, part):
    key_list = jax.random.split(key, 3)
    extent = (PENCIL_X, PENCIL_Y, SLOTS)
    values = jnp.clip(jax.random.normal(key_list[2], extent), -4.0, 4.0)
    return values.astype(jnp.float32)


def block_scale(key, shape, shards, smallest, top_value):
    def one(axis_at, blocks):
        draws = jax.random.uniform(jax.random.fold_in(jax.random.fold_in(key, 6), axis_at), (blocks,), jnp.float32, smallest / len(shards), top_value / len(shards))
        return jnp.repeat(jnp.exp(draws), shape[axis_at] // blocks).reshape((-1,) + (1,) * (len(shape) - axis_at - 1))

    level = one(*shards[0])
    for cut in shards[1:]:
        level = level * one(*cut)
    return level


def scatter_about(key, shape, deviation, reach, shards=(), dtype=jnp.bfloat16):
    array = deviation * jax.random.normal(key, shape, jnp.float32)
    if shards:
        array = array * block_scale(key, shape, shards, -0.22, 0.18)
    return jnp.clip(array, -reach, reach).astype(dtype)


def setup_inputs(seed: int = 0) -> dict:
    key_of = jax.random.split(jax.random.key(seed), 7)
    return {
        "atom_x": jnp.clip(23.99 * jax.random.uniform(key_of[0], (PENCIL_X, PENCIL_Y, SLOTS), jnp.float32) ** block_scale(key_of[0], (PENCIL_X, PENCIL_Y, SLOTS), ((0, 16), (1, 32)), -0.2, 0.2), 0.0, 23.99),
        "atom_y": jnp.clip(11.99 * jax.random.uniform(key_of[1], (PENCIL_X, PENCIL_Y, SLOTS), jnp.float32) ** block_scale(key_of[1], (PENCIL_X, PENCIL_Y, SLOTS), ((0, 16), (1, 32)), -0.2, 0.2), 0.0, 11.99),
        "atom_z": jnp.clip(384.0 * jax.random.uniform(key_of[2], (PENCIL_X, PENCIL_Y, SLOTS), jnp.float32) ** block_scale(key_of[2], (PENCIL_X, PENCIL_Y, SLOTS), ((0, 16), (1, 32)), -0.2, 0.2), 0.0, 384.0),
        "charges": draw_charges(jax.random.fold_in(key_of[6], 71), 0),
        "counts": draw_counts(jax.random.fold_in(key_of[6], 71), 0),
        "background": scatter_about(key_of[5], (NY, NX, NZ), 0.05, 0.3125, ((0, 32), (1, 16)), jnp.float32),
    }


COULOMB = 6.5
EWALD_BETA = 1.0
PRECISE = lax.Precision.HIGHEST


def spline(offset):
    distance = jnp.minimum(offset, 5.0 - offset)
    ramp_zero = jax.nn.relu(distance)
    ramp_one = jax.nn.relu(distance - 1.0)
    ramp_two = jax.nn.relu(distance - 2.0)
    cube_zero = ramp_zero * ramp_zero * ramp_zero
    cube_one = ramp_one * ramp_one * ramp_one
    cube_two = ramp_two * ramp_two * ramp_two
    height = (cube_zero * ramp_zero - 5.0 * cube_one * ramp_one + 10.0 * cube_two * ramp_two) / 24.0
    gradient = (cube_zero - 5.0 * cube_one + 10.0 * cube_two) / 6.0
    return height, jnp.where(offset < 2.5, gradient, -gradient)


def weights(coord_x, coord_y, coord_z, cells_x, cells_y, depth):
    edge_x = jnp.arange(cells_x + 4).astype(jnp.float32)
    weight_x, slope_x = spline(coord_x[None, :] - edge_x[:, None] + 4.5)
    edge_y = jnp.arange(cells_y + 4).astype(jnp.float32)
    weight_y, slope_y = spline(coord_y[None, :] - edge_y[:, None] + 4.5)
    planes = jnp.arange(depth).astype(jnp.float32)
    halfway = depth / 2.0
    offset_z = jnp.mod(coord_z[:, None] - planes[None, :] + halfway, float(depth)) - halfway + 2.5
    weight_z, slope_z = spline(offset_z)
    return weight_x, slope_x, weight_y, slope_y, weight_z, slope_z


def deposit(stencil, charge_live):
    weight_x, slope_x, weight_y, slope_y, weight_z, slope_z = stencil
    mixed = weight_y[:, None, :] * weight_x[None, :, :] * charge_live[None, None, :]
    flat = mixed.reshape(-1, charge_live.shape[0])
    spread = jnp.dot(flat, weight_z, precision=PRECISE, preferred_element_type=jnp.float32)
    return spread.reshape(weight_y.shape[0], weight_x.shape[0], weight_z.shape[1])


def pull(potential, stencil, charge_live):
    weight_x, slope_x, weight_y, slope_y, weight_z, slope_z = stencil
    extent_y, extent_x, depth = potential.shape
    flat = potential.reshape(extent_y * extent_x, depth)
    dims = (((1,), (1,)), ((), ()))
    plain = lax.dot_general(flat, weight_z, dims, precision=PRECISE, preferred_element_type=jnp.float32)
    deriv = lax.dot_general(flat, slope_z, dims, precision=PRECISE, preferred_element_type=jnp.float32)
    plain = plain.reshape(extent_y, extent_x, -1)
    deriv = deriv.reshape(extent_y, extent_x, -1)
    along_x = jnp.sum(weight_x[None] * plain, axis=1)
    turned_x = jnp.sum(slope_x[None] * plain, axis=1)
    depth_x = jnp.sum(weight_x[None] * deriv, axis=1)
    force_x = -charge_live * jnp.sum(weight_y * turned_x, axis=0)
    force_y = -charge_live * jnp.sum(slope_y * along_x, axis=0)
    force_z = -charge_live * jnp.sum(weight_y * depth_x, axis=0)
    return jnp.stack([force_x, force_y, force_z])


def modulus(indices, length):
    angles = (2.0 * math.pi / length) * indices.astype(jnp.float32)
    return (230.0 + 152.0 * jnp.cos(angles) + 2.0 * jnp.cos(2.0 * angles)) / 384.0


def frequency(indices, length):
    signed = jnp.where(indices <= length // 2, indices, indices - length)
    return signed.astype(jnp.float32) / length


def influence(wave_z, wave_x, wave_y, depth, width_x, width_y):
    freq_z = frequency(wave_z, depth)
    freq_x = frequency(wave_x, width_x)
    freq_y = frequency(wave_y, width_y)
    square = freq_z[:, None, None] ** 2 + freq_x[None, :, None] ** 2 + freq_y[None, None, :] ** 2
    damping = modulus(wave_z, depth)[:, None, None] * modulus(wave_x, width_x)[None, :, None] * modulus(wave_y, width_y)[None, None, :]
    bounded = jnp.where(square > 0.0, square, 1.0)
    factor = COULOMB / (math.pi * width_x * width_y * depth)
    green = factor * jnp.exp(-((math.pi / EWALD_BETA) ** 2) * square) / (bounded * damping * damping)
    return jnp.where(square > 0.0, green, 0.0)


def reference(atom_x, atom_y, atom_z, charges, counts, background):
    cells_x = NX // PENCIL_X
    cells_y = NY // PENCIL_Y
    pencils = PENCIL_X * PENCIL_Y
    slot_ids = jnp.arange(SLOTS).astype(jnp.int32)
    zero_index = jnp.zeros((), jnp.int32)

    def pencil_data(pencil):
        pencil = pencil.astype(jnp.int32)
        column = pencil // PENCIL_Y
        row_index = pencil % PENCIL_Y
        live = slot_ids < counts[column, row_index]
        charge_live = jnp.where(live, charges[column, row_index], 0.0)
        stencil = weights(atom_x[column, row_index], atom_y[column, row_index], atom_z[column, row_index], cells_x, cells_y, NZ)
        return column, row_index, charge_live, stencil

    def add_pencil(pencil, padded):
        column, row_index, charge_live, stencil = pencil_data(pencil)
        spread = deposit(stencil, charge_live)
        start_y = (row_index * cells_y).astype(jnp.int32)
        start_x = (column * cells_x).astype(jnp.int32)
        current = lax.dynamic_slice(padded, (start_y, start_x, zero_index), spread.shape)
        return lax.dynamic_update_slice(padded, current + spread, (start_y, start_x, zero_index))

    padded = lax.fori_loop(0, pencils, add_pencil, jnp.zeros((NY + 4, NX + 4, NZ), jnp.float32))
    rows_done = padded[2:NY + 2]
    rows_done = rows_done.at[:2].add(padded[NY + 2:]).at[NY - 2:].add(padded[:2])
    charge_grid = rows_done[:, 2:NX + 2]
    charge_grid = charge_grid.at[:, :2].add(rows_done[:, NX + 2:]).at[:, NX - 2:].add(rows_done[:, :2])
    charge_grid = charge_grid + background
    spectrum = jnp.fft.fftn(charge_grid)
    green = influence(jnp.arange(NZ).astype(jnp.int32), jnp.arange(NX).astype(jnp.int32), jnp.arange(NY).astype(jnp.int32), NZ, NX, NY)
    green = jnp.transpose(green, (2, 1, 0))
    potential = jnp.real(jnp.fft.ifftn(spectrum * green)) * float(NX * NY * NZ)
    wrapped = jnp.pad(potential, ((2, 2), (2, 2), (0, 0)), mode="wrap")

    def gather_pencil(pencil):
        column, row_index, charge_live, stencil = pencil_data(pencil)
        start_y = (row_index * cells_y).astype(jnp.int32)
        start_x = (column * cells_x).astype(jnp.int32)
        local = lax.dynamic_slice(wrapped, (start_y, start_x, zero_index), (cells_y + 4, cells_x + 4, NZ))
        return pull(local, stencil, charge_live)

    forces = lax.map(gather_pencil, jnp.arange(pencils).astype(jnp.int32))
    return forces.reshape(PENCIL_X, PENCIL_Y, 3, SLOTS).transpose(2, 0, 1, 3)
```

```python
import math

import jax
import jax.numpy as jnp
import ml_dtypes
import numpy as np
from jax import lax
from jax.experimental import pallas as pl
from jax.experimental.pallas import tpu as pltpu
from jax.sharding import PartitionSpec as P

COULOMB = 6.5
N = 384
RING = 16
ROWS = 32
CX, CY = N // RING, N // ROWS
EX, EY = 32, 16
KX = 28
SLOTS = 256
CHUNKS = 3
UNITS = 36
MESH = pl.DeviceIdType.MESH
F32 = jnp.float32
BF16 = jnp.bfloat16


def parts(table):
    high = table.astype(ml_dtypes.bfloat16)
    low = (table - high.astype(np.float64)).astype(ml_dtypes.bfloat16)
    return high, low


def cas(rows, columns):
    angles = (rows[:, None] * columns[None, :] % N) * (2.0 * math.pi / N)
    return np.cos(angles) + np.sin(angles)


def wide_table(table):
    high, low = parts(table)
    return np.concatenate([high, low, high], axis=1)


def tall_table(table):
    high, low = parts(table)
    return np.concatenate([high, low, high], axis=0)


def make_tables():
    wave = np.arange(N)
    along_z = wide_table(cas(wave, wave))
    inner_y = np.arange(EY)
    inner_y = np.where(inner_y < CY + 2, inner_y, inner_y - EY)
    cell_y = (inner_y[:, None] + CY * np.arange(ROWS)[None, :]).reshape(-1) % N
    ahead_y = tall_table(cas(cell_y, wave))
    back_y = tall_table(cas(wave, cell_y))
    inner_x = np.arange(EX)
    used = np.tile(inner_x < KX, RING)
    inner_x = np.where(inner_x < CX + 2, inner_x, inner_x - KX)
    cell_x = (CX * np.arange(RING)[:, None] + inner_x[None, :]).reshape(-1) % N
    matrix_x = cas(wave, cell_x) * used[None, :]
    ahead_x = wide_table(matrix_x)
    back_x = wide_table(matrix_x.T)
    signed = np.where(wave <= N // 2, wave, wave - N) / N
    angles = 2.0 * math.pi / N * wave
    modulus = (230.0 + 152.0 * np.cos(angles) + 2.0 * np.cos(2.0 * angles)) / 384.0
    decay = np.exp(-(math.pi**2) * signed**2) / modulus**2
    factor = COULOMB / (math.pi * N * N * N)
    green_x = np.broadcast_to(np.stack([decay, signed**2])[:, :, None], (2, N, 128))
    green_y = np.stack([decay * factor, signed**2]).reshape(2, 3, 1, 128)
    green_y = np.broadcast_to(green_y, (2, 3, 8, 128))
    return (
        along_z,
        ahead_y,
        back_y,
        ahead_x,
        back_x,
        np.ascontiguousarray(green_x, dtype=np.float32),
        np.ascontiguousarray(green_y, dtype=np.float32),
    )


def spline(offset):
    distance = jnp.minimum(offset, 5.0 - offset)
    ramp_zero = jnp.maximum(distance, 0.0)
    ramp_one = jnp.maximum(distance - 1.0, 0.0)
    ramp_two = jnp.maximum(distance - 2.0, 0.0)
    cube_zero = ramp_zero * ramp_zero * ramp_zero
    cube_one = ramp_one * ramp_one * ramp_one
    cube_two = ramp_two * ramp_two * ramp_two
    height = (cube_zero * ramp_zero - 5.0 * cube_one * ramp_one + 10.0 * cube_two * ramp_two) * (
        1.0 / 24.0
    )
    gradient = (cube_zero - 5.0 * cube_one + 10.0 * cube_two) * (1.0 / 6.0)
    return height, jnp.where(offset < 2.5, gradient, -gradient)


def halves(value):
    high = value.astype(BF16)
    return high, (value - high.astype(F32)).astype(BF16)


def dot(left, right):
    return jnp.dot(left, right, preferred_element_type=F32)


def dot_nt(left, right):
    return lax.dot_general(left, right, (((1,), (1,)), ((), ())), preferred_element_type=F32)


def exchange_blocks(items):
    lane = lax.broadcasted_iota(jnp.int32, (8, 128), 1)
    low = lane < 64
    even = (lane // 32) % 2 == 0

    def pair(first, second, shift, mask):
        back = pltpu.roll(second, shift, 1)
        ahead = pltpu.roll(first, 128 - shift, 1)
        return jnp.where(mask, first, back), jnp.where(mask, ahead, second)

    zero, two = pair(items[0], items[2], 64, low)
    one, three = pair(items[1], items[3], 64, low)
    zero, one = pair(zero, one, 32, even)
    two, three = pair(two, three, 32, even)
    return zero, one, two, three


def kernel(
    atom_x,
    atom_y,
    atom_z,
    charges,
    counts,
    background,
    table_z_hbm,
    ahead_y_hbm,
    back_y_hbm,
    ahead_x_hbm,
    back_x_hbm,
    green_x_hbm,
    green_y_hbm,
    out,
    table_z,
    ahead_y,
    back_y,
    ahead_x,
    back_x,
    green_x,
    green_y,
    table_sem,
    weight_z,
    slope_z,
    mixed,
    mixed_parts,
    charge,
    charge_parts,
    deposit_parts,
    pull_parts,
    lines,
    turned,
    spread_out,
    spread_in,
    wave_out,
    wave_in,
    back_out,
    back_in,
    cell_out,
    cell_in,
    gathered,
    send_one,
    recv_one,
    send_two,
    recv_two,
    send_three,
    recv_three,
    send_four,
    recv_four,
):
    ring = lax.axis_index("gx")
    major, minor = lax.axis_index("gy"), lax.axis_index("gz")
    row = major * 4 + minor
    core = lax.rem(minor, 2)

    def in_ring(index):
        return (index, major, minor)

    def in_rows(index):
        return (ring, lax.div(index, 4), lax.rem(index, 4))

    barrier = pltpu.get_barrier_semaphore()

    @pl.loop(1, ROWS)
    def _(step):
        pl.semaphore_signal(
            barrier, inc=1, device_id=in_rows(lax.rem(row + step, ROWS)), device_id_type=MESH
        )

    @pl.loop(1, RING)
    def _(step):
        pl.semaphore_signal(
            barrier, inc=1, device_id=in_ring(lax.rem(ring + step, RING)), device_id_type=MESH
        )

    tables = [
        pltpu.make_async_copy(source, target, table_sem.at[place])
        for place, (source, target) in enumerate(
            (
                (table_z_hbm, table_z),
                (ahead_y_hbm, ahead_y),
                (ahead_x_hbm, ahead_x),
                (green_x_hbm, green_x),
                (green_y_hbm, green_y),
                (back_x_hbm, back_x),
                (back_y_hbm, back_y),
            )
        )
    ]
    for copy in tables:
        copy.start()

    wave_in[:, :, KX:, :] = jnp.zeros((3, RING, EX - KX, 128), F32)
    back_in[:, KX:, :] = jnp.zeros((UNITS, EX - KX, 128), F32)

    slot = lax.broadcasted_iota(jnp.int32, (1, SLOTS), 1)
    live = jnp.where(slot < counts[0, 0], charges[0], 0.0)
    inner_y = lax.broadcasted_iota(jnp.int32, (EY, SLOTS), 0)
    inner_y = jnp.where(inner_y < CY + 2, inner_y, inner_y - EY).astype(F32)
    height_y, slope_y = spline(atom_y[0] - inner_y + 2.5)
    inner_x = lax.broadcasted_iota(jnp.int32, (EX, SLOTS), 0)
    used = inner_x < KX
    inner_x = jnp.where(inner_x < CX + 2, inner_x, inner_x - KX).astype(F32)
    height_x, slope_x = spline(atom_x[0] - inner_x + 2.5)
    height_x = jnp.where(used, height_x, 0.0)
    slope_x = jnp.where(used, slope_x, 0.0)

    @pl.loop(0, N // 64)
    def _(block):
        first = pl.multiple_of(block * 64, 64)
        plane = (lax.broadcasted_iota(jnp.int32, (64, SLOTS), 0) + first).astype(F32)
        offset = atom_z[0] - plane
        offset = jnp.where(offset >= N / 2.0, offset - N, offset)
        offset = jnp.where(offset < -N / 2.0, offset + N, offset)
        height, slope = spline(offset + 2.5)
        for value, target in ((height, weight_z), (slope, slope_z)):
            high, low = halves(value)
            target[pl.ds(first, 64), :] = high
            target[pl.ds(N + first, 64), :] = high
            target[pl.ds(2 * N + first, 64), :] = low

    charged_y = height_y * live
    for y in range(EY):
        for group in range(4):
            mixed[group * 128 + y * 8 : group * 128 + y * 8 + 8, :] = (
                height_x[group * 8 : group * 8 + 8] * charged_y[y : y + 1]
            )
    high, low = halves(mixed[...])
    mixed_parts[:, :SLOTS] = high
    mixed_parts[:, SLOTS : 2 * SLOTS] = high
    mixed_parts[:, 2 * SLOTS :] = low

    for group in range(3):
        for y in range(CY):
            charge[group * 128 + y * 8 : group * 128 + y * 8 + 8, :] = background[
                y, group * 8 : group * 8 + 8, :
            ]
        charge[group * 128 + CY * 8 : group * 128 + 128, :] = jnp.zeros((128 - CY * 8, N), F32)
    high, low = halves(charge[...])
    charge_parts[:, :N] = high
    charge_parts[:, N : 2 * N] = high
    charge_parts[:, 2 * N :] = low

    tables[0].wait()
    high, low = halves(dot(table_z[...], weight_z[...]))
    deposit_parts[:, :SLOTS] = high
    deposit_parts[:, SLOTS : 2 * SLOTS] = low
    deposit_parts[:, 2 * SLOTS :] = high
    for chunk in range(CHUNKS):
        for place, value in enumerate((high, low, high)):
            pull_parts[chunk, place * 128 : place * 128 + 128, :SLOTS] = value[
                chunk * 128 : chunk * 128 + 128
            ]

    pl.semaphore_wait(barrier, ROWS - 1 + RING - 1)

    spread_tiles = spread_out.reshape(CHUNKS, 4, 128, 128)

    @pl.loop(0, CHUNKS)
    def _(chunk):
        first = pl.multiple_of(chunk * 128, 128)
        atoms = dot_nt(deposit_parts[pl.ds(first, 128), :], mixed_parts[...])
        frozen = dot_nt(table_z[pl.ds(first, 128), :], charge_parts[...])
        for group in range(4):
            tile = atoms[:, group * 128 : group * 128 + 128]
            if group < 3:
                tile = tile + frozen[:, group * 128 : group * 128 + 128]
            spread_tiles[chunk, group] = tile
        pltpu.make_async_copy(
            spread_out.at[chunk, :, row], spread_in.at[chunk, :, :, row], recv_one.at[chunk]
        ).start()

        @pl.loop(1, ROWS)
        def _(step):
            target = lax.rem(row + step, ROWS)
            pltpu.make_async_remote_copy(
                spread_out.at[chunk, :, target],
                spread_in.at[chunk, :, :, row],
                send_one.at[chunk],
                recv_one.at[chunk],
                device_id=in_rows(target),
                device_id_type=MESH,
            ).start()

    high, low = halves(dot(table_z[...], slope_z[...]))
    for chunk in range(CHUNKS):
        for place, value in enumerate((high, low, high)):
            pull_parts[chunk, place * 128 : place * 128 + 128, SLOTS:] = value[
                chunk * 128 : chunk * 128 + 128
            ]

    tables[1].wait()
    spread_got = spread_in.reshape(CHUNKS, 4, 128, 128)

    @pl.loop(0, CHUNKS)
    def _(chunk):
        pltpu.make_async_copy(spread_in.at[chunk], spread_in.at[chunk], recv_one.at[chunk]).wait()
        for group in range(4):
            flipped = spread_got[chunk, group].T
            for quarter in range(4):
                items = [flipped[(quarter * 4 + j) * 8 : (quarter * 4 + j) * 8 + 8] for j in range(4)]
                for k, item in enumerate(exchange_blocks(items)):
                    lines[
                        k * EX + group * 8 : k * EX + group * 8 + 8,
                        quarter * 128 : quarter * 128 + 128,
                    ] = item
        high, low = halves(lines[...])
        waves = dot(jnp.concatenate([high, high, low], axis=1), ahead_y[...])
        for k in range(4):
            for tile in range(3):
                wave_out[chunk * 12 + k * 3 + tile] = waves[
                    k * EX : k * EX + EX, tile * 128 : tile * 128 + 128
                ]

        @pl.loop(0, 12)
        def _(step):
            unit = chunk * 12 + lax.rem(step + lax.div(3 * ring, 4), 12)
            target = lax.rem(5 * unit + 8 * core, RING)
            place = lax.div(unit, RING)

            @pl.when(target != ring)
            def _():
                pltpu.make_async_remote_copy(
                    wave_out.at[unit, 0:KX],
                    wave_in.at[place, ring, 0:KX],
                    send_two.at[unit],
                    recv_two.at[place],
                    device_id=in_ring(target),
                    device_id_type=MESH,
                ).start()

            @pl.when(target == ring)
            def _():
                pltpu.make_async_copy(
                    wave_out.at[unit, 0:KX], wave_in.at[place, ring, 0:KX], recv_two.at[place]
                ).start()

    for copy in tables[2:6]:
        copy.wait()
    base = lax.rem(13 * (ring + RING - 8 * core), RING)
    n_places = lax.div(UNITS - 1 - base, RING) + 1

    @pl.loop(0, n_places)
    def _(place):
        unit = place * RING + base
        pltpu.make_async_copy(
            wave_in.at[place, :, 0:KX], wave_in.at[place, :, 0:KX], recv_two.at[place]
        ).wait()
        high, low = halves(wave_in[place].reshape(RING * EX, 128))
        waves = dot(ahead_x[...], jnp.concatenate([high, high, low], axis=0))
        within = lax.rem(unit, 12)
        wave_z = lax.div(unit, 12) * 128 + row * 4 + lax.div(within, 3)
        tile = lax.rem(within, 3)
        decay = green_x[0, pl.ds(wave_z, 1), :] * green_y[0, tile]
        square = green_x[1, pl.ds(wave_z, 1), :] + green_y[1, tile]
        squares = green_x[1].reshape(N // 8, 8, 128) + square[None]
        decays = green_x[0].reshape(N // 8, 8, 128) * decay[None]
        green = jnp.where(squares > 0.0, decays / jnp.where(squares > 0.0, squares, 1.0), 0.0)
        high, low = halves(waves * green.reshape(N, 128))
        cells = dot(back_x[...], jnp.concatenate([high, high, low], axis=0))
        back_out[place] = cells.reshape(RING, EX, 128)
        group = lax.div(unit, 12)
        pltpu.make_async_copy(
            back_out.at[place, ring, 0:KX], back_in.at[unit, 0:KX], recv_three.at[group]
        ).start()

        @pl.loop(1, RING)
        def _(step):
            target = lax.rem(ring + step, RING)
            pltpu.make_async_remote_copy(
                back_out.at[place, target, 0:KX],
                back_in.at[unit, 0:KX],
                send_three.at[place, target],
                recv_three.at[group],
                device_id=in_ring(target),
                device_id_type=MESH,
            ).start()

    tables[6].wait()
    cell_tiles = cell_out.reshape(CHUNKS, 4, 128, 128)

    @pl.loop(0, CHUNKS)
    def _(chunk):
        units = pl.ds(chunk * 12, 12)
        pltpu.make_async_copy(
            back_in.at[units, 0:KX], back_in.at[units, 0:KX], recv_three.at[chunk]
        ).wait()
        tiles = [
            jnp.concatenate([back_in[chunk * 12 + k * 3 + tile] for tile in range(3)], axis=1)
            for k in range(4)
        ]
        high, low = halves(jnp.concatenate(tiles, axis=0))
        lines[...] = dot(jnp.concatenate([high, high, low], axis=1), back_y[...])
        for group in range(4):
            for quarter in range(4):
                items = [
                    lines[
                        k * EX + group * 8 : k * EX + group * 8 + 8,
                        quarter * 128 : quarter * 128 + 128,
                    ]
                    for k in range(4)
                ]
                for j, item in enumerate(exchange_blocks(items)):
                    turned[(quarter * 4 + j) * 8 : (quarter * 4 + j) * 8 + 8, :] = item
            cell_tiles[chunk, group] = turned[...].T
        pltpu.make_async_copy(
            cell_out.at[chunk, :, :, row], cell_in.at[chunk, :, row], recv_four.at[chunk]
        ).start()

        @pl.loop(1, ROWS)
        def _(step):
            target = lax.rem(row + step, ROWS)
            pltpu.make_async_remote_copy(
                cell_out.at[chunk, :, :, target],
                cell_in.at[chunk, :, row],
                send_four.at[chunk],
                recv_four.at[chunk],
                device_id=in_rows(target),
                device_id_type=MESH,
            ).start()

    cell_got = cell_in.reshape(CHUNKS, 4, 128, 128)
    gathered[...] = jnp.zeros((4 * 128, 2 * SLOTS), F32)

    @pl.loop(0, CHUNKS)
    def _(chunk):
        pltpu.make_async_copy(cell_in.at[chunk], cell_in.at[chunk], recv_four.at[chunk]).wait()
        for group in range(4):
            high, low = halves(cell_got[chunk, group].T)
            gathered[group * 128 : group * 128 + 128, :] += dot(
                jnp.concatenate([high, high, low], axis=1), pull_parts[chunk]
            )

    force_x = jnp.zeros((8, SLOTS), F32)
    force_y = jnp.zeros((8, SLOTS), F32)
    force_z = jnp.zeros((8, SLOTS), F32)
    for y in range(EY):
        along_x = jnp.zeros((8, SLOTS), F32)
        turned_x = jnp.zeros((8, SLOTS), F32)
        depth_x = jnp.zeros((8, SLOTS), F32)
        for group in range(4):
            first = group * 128 + y * 8
            plain = gathered[first : first + 8, :SLOTS]
            deriv = gathered[first : first + 8, SLOTS:]
            weight = height_x[group * 8 : group * 8 + 8]
            along_x += weight * plain
            turned_x += slope_x[group * 8 : group * 8 + 8] * plain
            depth_x += weight * deriv
        force_x += height_y[y : y + 1] * turned_x
        force_y += slope_y[y : y + 1] * along_x
        force_z += height_y[y : y + 1] * depth_x
    for place, force in enumerate((force_x, force_y, force_z)):
        out[place, 0] = -live * jnp.sum(force, axis=0, keepdims=True)

    @pl.loop(0, CHUNKS)
    def _(chunk):
        sizes = spread_out.at[chunk, :, 0 : ROWS - 1]
        pltpu.make_async_copy(sizes, sizes, send_one.at[chunk]).wait()
        sizes = cell_in.at[chunk, :, 0 : ROWS - 1]
        pltpu.make_async_copy(sizes, sizes, send_four.at[chunk]).wait()

    @pl.loop(0, UNITS)
    def _(unit):
        @pl.when(lax.rem(5 * unit + 8 * core, RING) != ring)
        def _():
            sizes = wave_out.at[unit, 0:KX]
            pltpu.make_async_copy(sizes, sizes, send_two.at[unit]).wait()

    @pl.loop(0, n_places)
    def _(place):
        @pl.loop(1, RING)
        def _(step):
            target = lax.rem(ring + step, RING)
            sizes = back_out.at[place, target, 0:KX]
            pltpu.make_async_copy(sizes, sizes, send_three.at[place, target]).wait()


def solution(mesh):
    tables = make_tables()

    def per_device(*args):
        vmem = pl.BlockSpec(memory_space=pltpu.VMEM)
        anywhere = pl.BlockSpec(memory_space=pl.ANY)
        held = [pltpu.VMEM(tables[place].shape, tables[place].dtype) for place in range(7)]
        return pl.pallas_call(
            kernel,
            out_shape=jax.ShapeDtypeStruct((3, 1, 1, SLOTS), F32),
            in_specs=[vmem] * 4 + [pl.BlockSpec(memory_space=pltpu.SMEM), vmem] + [anywhere] * 7,
            out_specs=vmem,
            scratch_shapes=held
            + [
                pltpu.SemaphoreType.DMA((7,)),
                pltpu.VMEM((3 * N, SLOTS), BF16),
                pltpu.VMEM((3 * N, SLOTS), BF16),
                pltpu.VMEM((4 * 128, SLOTS), F32),
                pltpu.VMEM((4 * 128, 3 * SLOTS), BF16),
                pltpu.VMEM((3 * 128, N), F32),
                pltpu.VMEM((3 * 128, 3 * N), BF16),
                pltpu.VMEM((N, 3 * SLOTS), BF16),
                pltpu.VMEM((CHUNKS, 3 * 128, 2 * SLOTS), BF16),
                pltpu.VMEM((4 * EX, EY * ROWS), F32),
                pltpu.VMEM((128, 128), F32),
                pltpu.VMEM((CHUNKS, 4, ROWS, 4, 1, 128), F32),
                pltpu.VMEM((CHUNKS, 4, 4, ROWS, 1, 128), F32),
                pltpu.VMEM((UNITS, EX, 128), F32),
                pltpu.VMEM((3, RING, EX, 128), F32),
                pltpu.VMEM((3, RING, EX, 128), F32),
                pltpu.VMEM((UNITS, EX, 128), F32),
                pltpu.VMEM((CHUNKS, 4, 4, ROWS, 1, 128), F32),
                pltpu.VMEM((CHUNKS, 4, ROWS, 4, 1, 128), F32),
                pltpu.VMEM((4 * 128, 2 * SLOTS), F32),
                pltpu.SemaphoreType.DMA((CHUNKS,)),
                pltpu.SemaphoreType.DMA((CHUNKS,)),
                pltpu.SemaphoreType.DMA((UNITS,)),
                pltpu.SemaphoreType.DMA((3,)),
                pltpu.SemaphoreType.DMA((3, RING)),
                pltpu.SemaphoreType.DMA((CHUNKS,)),
                pltpu.SemaphoreType.DMA((CHUNKS,)),
                pltpu.SemaphoreType.DMA((CHUNKS,)),
            ],
            compiler_params=pltpu.CompilerParams(
                collective_id=0, has_side_effects=True, vmem_limit_bytes=40 * 1024 * 1024
            ),
            name="ewald",
        )(*args, *(jnp.asarray(table) for table in tables))

    pencils = P("gx", ("gy", "gz"), None)
    return jax.shard_map(
        per_device,
        mesh=mesh,
        in_specs=(pencils,) * 4 + (P("gx", ("gy", "gz")), P(("gy", "gz"), "gx", None)),
        out_specs=P(None, "gx", ("gy", "gz"), None),
        check_vma=False,
    )
```

```python
import math

import jax
import jax.numpy as jnp
import ml_dtypes
import numpy as np
from jax import lax
from jax.experimental import pallas as pl
from jax.experimental.pallas import tpu as pltpu
from jax.sharding import PartitionSpec as P

COULOMB = 6.5
N = 384
RING = 16
ROWS = 32
CX, CY = N // RING, N // ROWS
EX, EY = 32, 16
KX = 28
SLOTS = 256
CHUNKS = 3
UNITS = 36
MESH = pl.DeviceIdType.MESH
F32 = jnp.float32
BF16 = jnp.bfloat16


def parts(table):
    high = table.astype(ml_dtypes.bfloat16)
    low = (table - high.astype(np.float64)).astype(ml_dtypes.bfloat16)
    return high, low


def cas(rows, columns):
    angles = (rows[:, None] * columns[None, :] % N) * (2.0 * math.pi / N)
    return np.cos(angles) + np.sin(angles)


def wide_table(table):
    high, low = parts(table)
    return np.concatenate([high, low, high], axis=1)


def tall_table(table):
    high, low = parts(table)
    return np.concatenate([high, low, high], axis=0)


def make_tables():
    wave = np.arange(N)
    along_z = wide_table(cas(wave, wave))
    inner_y = np.arange(EY)
    inner_y = np.where(inner_y < CY + 2, inner_y, inner_y - EY)
    cell_y = (inner_y[:, None] + CY * np.arange(ROWS)[None, :]).reshape(-1) % N
    ahead_y = tall_table(cas(cell_y, wave))
    back_y = tall_table(cas(wave, cell_y))
    inner_x = np.arange(EX)
    used = np.tile(inner_x < KX, RING)
    inner_x = np.where(inner_x < CX + 2, inner_x, inner_x - KX)
    cell_x = (CX * np.arange(RING)[:, None] + inner_x[None, :]).reshape(-1) % N
    matrix_x = cas(wave, cell_x) * used[None, :]
    ahead_x = wide_table(matrix_x)
    back_x = wide_table(matrix_x.T)
    signed = np.where(wave <= N // 2, wave, wave - N) / N
    angles = 2.0 * math.pi / N * wave
    modulus = (230.0 + 152.0 * np.cos(angles) + 2.0 * np.cos(2.0 * angles)) / 384.0
    decay = np.exp(-(math.pi**2) * signed**2) / modulus**2
    factor = COULOMB / (math.pi * N * N * N)
    green_x = np.broadcast_to(np.stack([decay, signed**2])[:, :, None], (2, N, 128))
    green_y = np.stack([decay * factor, signed**2]).reshape(2, 3, 1, 128)
    green_y = np.broadcast_to(green_y, (2, 3, 8, 128))
    return (
        along_z,
        ahead_y,
        back_y,
        ahead_x,
        back_x,
        np.ascontiguousarray(green_x, dtype=np.float32),
        np.ascontiguousarray(green_y, dtype=np.float32),
    )


def spline(offset):
    distance = jnp.minimum(offset, 5.0 - offset)
    ramp_zero = jnp.maximum(distance, 0.0)
    ramp_one = jnp.maximum(distance - 1.0, 0.0)
    ramp_two = jnp.maximum(distance - 2.0, 0.0)
    cube_zero = ramp_zero * ramp_zero * ramp_zero
    cube_one = ramp_one * ramp_one * ramp_one
    cube_two = ramp_two * ramp_two * ramp_two
    height = (cube_zero * ramp_zero - 5.0 * cube_one * ramp_one + 10.0 * cube_two * ramp_two) * (
        1.0 / 24.0
    )
    gradient = (cube_zero - 5.0 * cube_one + 10.0 * cube_two) * (1.0 / 6.0)
    return height, jnp.where(offset < 2.5, gradient, -gradient)


def halves(value):
    high = value.astype(BF16)
    return high, (value - high.astype(F32)).astype(BF16)


def dot(left, right):
    return jnp.dot(left, right, preferred_element_type=F32)


def dot_nt(left, right):
    return lax.dot_general(left, right, (((1,), (1,)), ((), ())), preferred_element_type=F32)


def exchange_blocks(items):
    lane = lax.broadcasted_iota(jnp.int32, (8, 128), 1)
    low = lane < 64
    even = (lane // 32) % 2 == 0

    def pair(first, second, shift, mask):
        back = pltpu.roll(second, shift, 1)
        ahead = pltpu.roll(first, 128 - shift, 1)
        return jnp.where(mask, first, back), jnp.where(mask, ahead, second)

    zero, two = pair(items[0], items[2], 64, low)
    one, three = pair(items[1], items[3], 64, low)
    zero, one = pair(zero, one, 32, even)
    two, three = pair(two, three, 32, even)
    return zero, one, two, three


def kernel(
    atom_x_hbm,
    atom_y_hbm,
    atom_z_hbm,
    charges_hbm,
    counts,
    background_hbm,
    table_z_hbm,
    ahead_y_hbm,
    back_y_hbm,
    ahead_x_hbm,
    back_x_hbm,
    green_x_hbm,
    green_y_hbm,
    out,
    atom_x,
    atom_y,
    atom_z,
    charges,
    background,
    table_z,
    ahead_y,
    back_y,
    ahead_x,
    back_x,
    green_x,
    green_y,
    table_sem,
    weight_z,
    slope_z,
    mixed,
    mixed_parts,
    charge,
    charge_parts,
    deposit_parts,
    pull_parts,
    lines,
    turned,
    spread_out,
    spread_in,
    wave_out,
    wave_in,
    back_out,
    back_in,
    cell_out,
    cell_in,
    gathered,
    send_one,
    recv_one,
    send_two,
    recv_two,
    send_three,
    recv_three,
    send_four,
    recv_four,
):
    ring = lax.axis_index("gx")
    major, minor = lax.axis_index("gy"), lax.axis_index("gz")
    row = major * 4 + minor
    core = lax.rem(minor, 2)

    def in_ring(index):
        return (index, major, minor)

    def in_rows(index):
        return (ring, lax.div(index, 4), lax.rem(index, 4))

    barrier = pltpu.get_barrier_semaphore()

    @pl.loop(1, ROWS)
    def _(step):
        pl.semaphore_signal(
            barrier, inc=1, device_id=in_rows(lax.rem(row + step, ROWS)), device_id_type=MESH
        )

    @pl.loop(1, RING)
    def _(step):
        pl.semaphore_signal(
            barrier, inc=1, device_id=in_ring(lax.rem(ring + step, RING)), device_id_type=MESH
        )

    tables = [
        pltpu.make_async_copy(source, target, table_sem.at[place])
        for place, (source, target) in enumerate(
            (
                (atom_x_hbm, atom_x),
                (atom_y_hbm, atom_y),
                (atom_z_hbm, atom_z),
                (charges_hbm, charges),
                (table_z_hbm, table_z),
                (background_hbm, background),
                (ahead_y_hbm, ahead_y),
                (ahead_x_hbm, ahead_x),
                (green_x_hbm, green_x),
                (green_y_hbm, green_y),
                (back_x_hbm, back_x),
                (back_y_hbm, back_y),
            )
        )
    ]
    for copy in tables:
        copy.start()

    wave_in[:, :, KX:, :] = jnp.zeros((3, RING, EX - KX, 128), F32)
    back_in[:, KX:, :] = jnp.zeros((UNITS, EX - KX, 128), F32)

    for copy in tables[:4]:
        copy.wait()
    slot = lax.broadcasted_iota(jnp.int32, (1, SLOTS), 1)
    live = jnp.where(slot < counts[0, 0], charges[0], 0.0)
    inner_y = lax.broadcasted_iota(jnp.int32, (EY, SLOTS), 0)
    inner_y = jnp.where(inner_y < CY + 2, inner_y, inner_y - EY).astype(F32)
    height_y, slope_y = spline(atom_y[0] - inner_y + 2.5)
    inner_x = lax.broadcasted_iota(jnp.int32, (EX, SLOTS), 0)
    used = inner_x < KX
    inner_x = jnp.where(inner_x < CX + 2, inner_x, inner_x - KX).astype(F32)
    height_x, slope_x = spline(atom_x[0] - inner_x + 2.5)
    height_x = jnp.where(used, height_x, 0.0)
    slope_x = jnp.where(used, slope_x, 0.0)

    @pl.loop(0, N // 64)
    def _(block):
        first = pl.multiple_of(block * 64, 64)
        plane = (lax.broadcasted_iota(jnp.int32, (64, SLOTS), 0) + first).astype(F32)
        offset = atom_z[0] - plane
        offset = jnp.where(offset >= N / 2.0, offset - N, offset)
        offset = jnp.where(offset < -N / 2.0, offset + N, offset)
        height, slope = spline(offset + 2.5)
        for value, target in ((height, weight_z), (slope, slope_z)):
            high, low = halves(value)
            target[pl.ds(first, 64), :] = high
            target[pl.ds(N + first, 64), :] = high
            target[pl.ds(2 * N + first, 64), :] = low

    charged_y = height_y * live
    for y in range(EY):
        for group in range(4):
            mixed[group * 128 + y * 8 : group * 128 + y * 8 + 8, :] = (
                height_x[group * 8 : group * 8 + 8] * charged_y[y : y + 1]
            )
    high, low = halves(mixed[...])
    mixed_parts[:, :SLOTS] = high
    mixed_parts[:, SLOTS : 2 * SLOTS] = high
    mixed_parts[:, 2 * SLOTS :] = low

    tables[5].wait()
    for group in range(3):
        for y in range(CY):
            charge[group * 128 + y * 8 : group * 128 + y * 8 + 8, :] = background[
                y, group * 8 : group * 8 + 8, :
            ]
        charge[group * 128 + CY * 8 : group * 128 + 128, :] = jnp.zeros((128 - CY * 8, N), F32)
    high, low = halves(charge[...])
    charge_parts[:, :N] = high
    charge_parts[:, N : 2 * N] = high
    charge_parts[:, 2 * N :] = low

    tables[4].wait()
    high, low = halves(dot(table_z[...], weight_z[...]))
    deposit_parts[:, :SLOTS] = high
    deposit_parts[:, SLOTS : 2 * SLOTS] = low
    deposit_parts[:, 2 * SLOTS :] = high
    for chunk in range(CHUNKS):
        for place, value in enumerate((high, low, high)):
            pull_parts[chunk, place * 128 : place * 128 + 128, :SLOTS] = value[
                chunk * 128 : chunk * 128 + 128
            ]

    pl.semaphore_wait(barrier, ROWS - 1 + RING - 1)

    spread_tiles = spread_out.reshape(CHUNKS, 4, 128, 128)

    @pl.loop(0, CHUNKS)
    def _(chunk):
        first = pl.multiple_of(chunk * 128, 128)
        atoms = dot_nt(deposit_parts[pl.ds(first, 128), :], mixed_parts[...])
        frozen = dot_nt(table_z[pl.ds(first, 128), :], charge_parts[...])
        for group in range(4):
            tile = atoms[:, group * 128 : group * 128 + 128]
            if group < 3:
                tile = tile + frozen[:, group * 128 : group * 128 + 128]
            spread_tiles[chunk, group] = tile
        pltpu.make_async_copy(
            spread_out.at[chunk, :, row], spread_in.at[chunk, :, :, row], recv_one.at[chunk]
        ).start()

        @pl.loop(1, ROWS)
        def _(step):
            target = lax.rem(row + step, ROWS)
            pltpu.make_async_remote_copy(
                spread_out.at[chunk, :, target],
                spread_in.at[chunk, :, :, row],
                send_one.at[chunk],
                recv_one.at[chunk],
                device_id=in_rows(target),
                device_id_type=MESH,
            ).start()

    high, low = halves(dot(table_z[...], slope_z[...]))
    for chunk in range(CHUNKS):
        for place, value in enumerate((high, low, high)):
            pull_parts[chunk, place * 128 : place * 128 + 128, SLOTS:] = value[
                chunk * 128 : chunk * 128 + 128
            ]

    tables[6].wait()
    spread_got = spread_in.reshape(CHUNKS, 4, 128, 128)

    @pl.loop(0, CHUNKS)
    def _(chunk):
        pltpu.make_async_copy(spread_in.at[chunk], spread_in.at[chunk], recv_one.at[chunk]).wait()
        for group in range(4):
            flipped = spread_got[chunk, group].T
            for quarter in range(4):
                items = [flipped[(quarter * 4 + j) * 8 : (quarter * 4 + j) * 8 + 8] for j in range(4)]
                for k, item in enumerate(exchange_blocks(items)):
                    lines[
                        k * EX + group * 8 : k * EX + group * 8 + 8,
                        quarter * 128 : quarter * 128 + 128,
                    ] = item
        high, low = halves(lines[...])
        waves = dot(jnp.concatenate([high, high, low], axis=1), ahead_y[...])
        for k in range(4):
            for tile in range(3):
                wave_out[chunk * 12 + k * 3 + tile] = waves[
                    k * EX : k * EX + EX, tile * 128 : tile * 128 + 128
                ]

        @pl.loop(0, 12)
        def _(step):
            unit = chunk * 12 + lax.rem(step + lax.div(3 * ring, 4), 12)
            target = lax.rem(5 * unit + 8 * core, RING)
            place = lax.div(unit, RING)

            @pl.when(target != ring)
            def _():
                pltpu.make_async_remote_copy(
                    wave_out.at[unit, 0:KX],
                    wave_in.at[place, ring, 0:KX],
                    send_two.at[unit],
                    recv_two.at[place],
                    device_id=in_ring(target),
                    device_id_type=MESH,
                ).start()

            @pl.when(target == ring)
            def _():
                pltpu.make_async_copy(
                    wave_out.at[unit, 0:KX], wave_in.at[place, ring, 0:KX], recv_two.at[place]
                ).start()

    for copy in tables[7:11]:
        copy.wait()
    base = lax.rem(13 * (ring + RING - 8 * core), RING)
    n_places = lax.div(UNITS - 1 - base, RING) + 1

    @pl.loop(0, n_places)
    def _(place):
        unit = place * RING + base
        pltpu.make_async_copy(
            wave_in.at[place, :, 0:KX], wave_in.at[place, :, 0:KX], recv_two.at[place]
        ).wait()
        high, low = halves(wave_in[place].reshape(RING * EX, 128))
        waves = dot(ahead_x[...], jnp.concatenate([high, high, low], axis=0))
        within = lax.rem(unit, 12)
        wave_z = lax.div(unit, 12) * 128 + row * 4 + lax.div(within, 3)
        tile = lax.rem(within, 3)
        decay = green_x[0, pl.ds(wave_z, 1), :] * green_y[0, tile]
        square = green_x[1, pl.ds(wave_z, 1), :] + green_y[1, tile]
        squares = green_x[1].reshape(N // 8, 8, 128) + square[None]
        decays = green_x[0].reshape(N // 8, 8, 128) * decay[None]
        green = jnp.where(squares > 0.0, decays / jnp.where(squares > 0.0, squares, 1.0), 0.0)
        high, low = halves(waves * green.reshape(N, 128))
        cells = dot(back_x[...], jnp.concatenate([high, high, low], axis=0))
        back_out[place] = cells.reshape(RING, EX, 128)
        group = lax.div(unit, 12)
        pltpu.make_async_copy(
            back_out.at[place, ring, 0:KX], back_in.at[unit, 0:KX], recv_three.at[group]
        ).start()

        @pl.loop(1, RING)
        def _(step):
            target = lax.rem(ring + step, RING)
            pltpu.make_async_remote_copy(
                back_out.at[place, target, 0:KX],
                back_in.at[unit, 0:KX],
                send_three.at[place, target],
                recv_three.at[group],
                device_id=in_ring(target),
                device_id_type=MESH,
            ).start()

    tables[11].wait()
    cell_tiles = cell_out.reshape(CHUNKS, 4, 128, 128)

    @pl.loop(0, CHUNKS)
    def _(chunk):
        units = pl.ds(chunk * 12, 12)
        pltpu.make_async_copy(
            back_in.at[units, 0:KX], back_in.at[units, 0:KX], recv_three.at[chunk]
        ).wait()
        tiles = [
            jnp.concatenate([back_in[chunk * 12 + k * 3 + tile] for tile in range(3)], axis=1)
            for k in range(4)
        ]
        high, low = halves(jnp.concatenate(tiles, axis=0))
        lines[...] = dot(jnp.concatenate([high, high, low], axis=1), back_y[...])
        for group in range(4):
            for quarter in range(4):
                items = [
                    lines[
                        k * EX + group * 8 : k * EX + group * 8 + 8,
                        quarter * 128 : quarter * 128 + 128,
                    ]
                    for k in range(4)
                ]
                for j, item in enumerate(exchange_blocks(items)):
                    turned[(quarter * 4 + j) * 8 : (quarter * 4 + j) * 8 + 8, :] = item
            cell_tiles[chunk, group] = turned[...].T
        pltpu.make_async_copy(
            cell_out.at[chunk, :, :, row], cell_in.at[chunk, :, row], recv_four.at[chunk]
        ).start()

        @pl.loop(1, ROWS)
        def _(step):
            target = lax.rem(row + step, ROWS)
            pltpu.make_async_remote_copy(
                cell_out.at[chunk, :, :, target],
                cell_in.at[chunk, :, row],
                send_four.at[chunk],
                recv_four.at[chunk],
                device_id=in_rows(target),
                device_id_type=MESH,
            ).start()

    cell_got = cell_in.reshape(CHUNKS, 4, 128, 128)
    gathered[...] = jnp.zeros((4 * 128, 2 * SLOTS), F32)

    @pl.loop(0, CHUNKS)
    def _(chunk):
        pltpu.make_async_copy(cell_in.at[chunk], cell_in.at[chunk], recv_four.at[chunk]).wait()
        for group in range(4):
            high, low = halves(cell_got[chunk, group].T)
            gathered[group * 128 : group * 128 + 128, :] += dot(
                jnp.concatenate([high, high, low], axis=1), pull_parts[chunk]
            )

    force_x = jnp.zeros((8, SLOTS), F32)
    force_y = jnp.zeros((8, SLOTS), F32)
    force_z = jnp.zeros((8, SLOTS), F32)
    for y in range(EY):
        along_x = jnp.zeros((8, SLOTS), F32)
        turned_x = jnp.zeros((8, SLOTS), F32)
        depth_x = jnp.zeros((8, SLOTS), F32)
        for group in range(4):
            first = group * 128 + y * 8
            plain = gathered[first : first + 8, :SLOTS]
            deriv = gathered[first : first + 8, SLOTS:]
            weight = height_x[group * 8 : group * 8 + 8]
            along_x += weight * plain
            turned_x += slope_x[group * 8 : group * 8 + 8] * plain
            depth_x += weight * deriv
        force_x += height_y[y : y + 1] * turned_x
        force_y += slope_y[y : y + 1] * along_x
        force_z += height_y[y : y + 1] * depth_x
    for place, force in enumerate((force_x, force_y, force_z)):
        out[place, 0] = -live * jnp.sum(force, axis=0, keepdims=True)

    @pl.loop(0, CHUNKS)
    def _(chunk):
        sizes = spread_out.at[chunk, :, 0 : ROWS - 1]
        pltpu.make_async_copy(sizes, sizes, send_one.at[chunk]).wait()
        sizes = cell_in.at[chunk, :, 0 : ROWS - 1]
        pltpu.make_async_copy(sizes, sizes, send_four.at[chunk]).wait()

    @pl.loop(0, UNITS)
    def _(unit):
        @pl.when(lax.rem(5 * unit + 8 * core, RING) != ring)
        def _():
            sizes = wave_out.at[unit, 0:KX]
            pltpu.make_async_copy(sizes, sizes, send_two.at[unit]).wait()

    @pl.loop(0, n_places)
    def _(place):
        @pl.loop(1, RING)
        def _(step):
            target = lax.rem(ring + step, RING)
            sizes = back_out.at[place, target, 0:KX]
            pltpu.make_async_copy(sizes, sizes, send_three.at[place, target]).wait()


def solution(mesh):
    tables = make_tables()

    def per_device(*args):
        vmem = pl.BlockSpec(memory_space=pltpu.VMEM)
        anywhere = pl.BlockSpec(memory_space=pl.ANY)
        held = [pltpu.VMEM(value.shape, value.dtype) for value in (*args[:4], args[5], *tables)]
        return pl.pallas_call(
            kernel,
            out_shape=jax.ShapeDtypeStruct((3, 1, 1, SLOTS), F32),
            in_specs=[anywhere] * 4 + [pl.BlockSpec(memory_space=pltpu.SMEM)] + [anywhere] * 8,
            out_specs=vmem,
            scratch_shapes=held
            + [
                pltpu.SemaphoreType.DMA((12,)),
                pltpu.VMEM((3 * N, SLOTS), BF16),
                pltpu.VMEM((3 * N, SLOTS), BF16),
                pltpu.VMEM((4 * 128, SLOTS), F32),
                pltpu.VMEM((4 * 128, 3 * SLOTS), BF16),
                pltpu.VMEM((3 * 128, N), F32),
                pltpu.VMEM((3 * 128, 3 * N), BF16),
                pltpu.VMEM((N, 3 * SLOTS), BF16),
                pltpu.VMEM((CHUNKS, 3 * 128, 2 * SLOTS), BF16),
                pltpu.VMEM((4 * EX, EY * ROWS), F32),
                pltpu.VMEM((128, 128), F32),
                pltpu.VMEM((CHUNKS, 4, ROWS, 4, 1, 128), F32),
                pltpu.VMEM((CHUNKS, 4, 4, ROWS, 1, 128), F32),
                pltpu.VMEM((UNITS, EX, 128), F32),
                pltpu.VMEM((3, RING, EX, 128), F32),
                pltpu.VMEM((3, RING, EX, 128), F32),
                pltpu.VMEM((UNITS, EX, 128), F32),
                pltpu.VMEM((CHUNKS, 4, 4, ROWS, 1, 128), F32),
                pltpu.VMEM((CHUNKS, 4, ROWS, 4, 1, 128), F32),
                pltpu.VMEM((4 * 128, 2 * SLOTS), F32),
                pltpu.SemaphoreType.DMA((CHUNKS,)),
                pltpu.SemaphoreType.DMA((CHUNKS,)),
                pltpu.SemaphoreType.DMA((UNITS,)),
                pltpu.SemaphoreType.DMA((3,)),
                pltpu.SemaphoreType.DMA((3, RING)),
                pltpu.SemaphoreType.DMA((CHUNKS,)),
                pltpu.SemaphoreType.DMA((CHUNKS,)),
                pltpu.SemaphoreType.DMA((CHUNKS,)),
            ],
            compiler_params=pltpu.CompilerParams(
                collective_id=0, has_side_effects=True, vmem_limit_bytes=60 * 1024 * 1024
            ),
            name="ewald",
        )(*args, *(jnp.asarray(table) for table in tables))

    pencils = P("gx", ("gy", "gz"), None)
    return jax.shard_map(
        per_device,
        mesh=mesh,
        in_specs=(pencils,) * 4 + (P("gx", ("gy", "gz")), P(("gy", "gz"), "gx", None)),
        out_specs=P(None, "gx", ("gy", "gz"), None),
        check_vma=False,
    )
```

```python
import math

import jax
import jax.numpy as jnp
import ml_dtypes
import numpy as np
from jax import lax
from jax.experimental import pallas as pl
from jax.experimental.pallas import tpu as pltpu
from jax.sharding import PartitionSpec as P

COULOMB = 6.5
N = 384
RING = 16
ROWS = 32
CX, CY = N // RING, N // ROWS
EY = 16
GROUPS = CX // 8
MAIN = GROUPS * 128
EDGE = 64
SLOTS = 256
CHUNKS = 3
UNITS = 36
MESH = pl.DeviceIdType.MESH
F32 = jnp.float32
BF16 = jnp.bfloat16


def parts(table):
    high = table.astype(ml_dtypes.bfloat16)
    low = (table - high.astype(np.float64)).astype(ml_dtypes.bfloat16)
    return high, low


def cas(rows, columns):
    angles = (rows[:, None] * columns[None, :] % N) * (2.0 * math.pi / N)
    return np.cos(angles) + np.sin(angles)


def wide_table(table):
    high, low = parts(table)
    return np.concatenate([high, low, high], axis=1)


def tall_table(table):
    high, low = parts(table)
    return np.concatenate([high, low, high], axis=0)


def make_tables():
    wave = np.arange(N)
    along = wide_table(cas(wave, wave))
    inner_y = np.arange(EY)
    inner_y = np.where(inner_y < CY + 2, inner_y, inner_y - EY)
    cell_y = (inner_y[:, None] + CY * np.arange(ROWS)[None, :]).reshape(-1) % N
    ahead_y = tall_table(cas(cell_y, wave))
    back_y = tall_table(cas(wave, cell_y))
    signed = np.where(wave <= N // 2, wave, wave - N) / N
    angles = 2.0 * math.pi / N * wave
    modulus = (230.0 + 152.0 * np.cos(angles) + 2.0 * np.cos(2.0 * angles)) / 384.0
    decay = np.exp(-(math.pi**2) * signed**2) / modulus**2
    factor = COULOMB / (math.pi * N * N * N)
    green_x = np.broadcast_to(np.stack([decay, signed**2])[:, :, None], (2, N, 128))
    green_y = np.stack([decay * factor, signed**2]).reshape(2, 3, 1, 128)
    green_y = np.broadcast_to(green_y, (2, 3, 8, 128))
    return (
        along,
        ahead_y,
        back_y,
        np.ascontiguousarray(green_x, dtype=np.float32),
        np.ascontiguousarray(green_y, dtype=np.float32),
    )


def spline(offset):
    distance = jnp.minimum(offset, 5.0 - offset)
    ramp_zero = jnp.maximum(distance, 0.0)
    ramp_one = jnp.maximum(distance - 1.0, 0.0)
    ramp_two = jnp.maximum(distance - 2.0, 0.0)
    cube_zero = ramp_zero * ramp_zero * ramp_zero
    cube_one = ramp_one * ramp_one * ramp_one
    cube_two = ramp_two * ramp_two * ramp_two
    height = (cube_zero * ramp_zero - 5.0 * cube_one * ramp_one + 10.0 * cube_two * ramp_two) * (
        1.0 / 24.0
    )
    gradient = (cube_zero - 5.0 * cube_one + 10.0 * cube_two) * (1.0 / 6.0)
    return height, jnp.where(offset < 2.5, gradient, -gradient)


def halves(value):
    high = value.astype(BF16)
    return high, (value - high.astype(F32)).astype(BF16)


def dot(left, right):
    return jnp.dot(left, right, preferred_element_type=F32)


def dot_nt(left, right):
    return lax.dot_general(left, right, (((1,), (1,)), ((), ())), preferred_element_type=F32)


def exchange_blocks(items):
    lane = lax.broadcasted_iota(jnp.int32, (8, 128), 1)
    low = lane < 64
    even = (lane // 32) % 2 == 0

    def pair(first, second, shift, mask):
        back = pltpu.roll(second, shift, 1)
        ahead = pltpu.roll(first, 128 - shift, 1)
        return jnp.where(mask, first, back), jnp.where(mask, ahead, second)

    zero, two = pair(items[0], items[2], 64, low)
    one, three = pair(items[1], items[3], 64, low)
    zero, one = pair(zero, one, 32, even)
    two, three = pair(two, three, 32, even)
    return zero, one, two, three


def kernel(
    atom_x_hbm,
    atom_y_hbm,
    atom_z_hbm,
    charges_hbm,
    counts,
    background_hbm,
    table_hbm,
    ahead_y_hbm,
    back_y_hbm,
    green_x_hbm,
    green_y_hbm,
    out,
    atom_x,
    atom_y,
    atom_z,
    charges,
    background,
    table,
    ahead_y,
    back_y,
    green_x,
    green_y,
    table_sem,
    weight_z,
    slope_z,
    mixed,
    mixed_parts,
    charge,
    charge_parts,
    deposit_parts,
    pull_parts,
    lines,
    turned,
    spread_out,
    spread_in,
    wave_out,
    wave_in,
    back_out,
    back_in,
    cell_out,
    cell_in,
    halo_out,
    halo_in,
    flank_out,
    flank_in,
    cells,
    gathered,
    send_one,
    recv_one,
    send_two,
    recv_two,
    send_three,
    recv_three,
    send_four,
    recv_four,
    send_halo,
    recv_halo,
    send_flank,
    recv_flank,
):
    ring = lax.axis_index("gx")
    major, minor = lax.axis_index("gy"), lax.axis_index("gz")
    row = major * 4 + minor
    core = lax.rem(minor, 2)

    def in_ring(index):
        return (index, major, minor)

    def in_rows(index):
        return (ring, lax.div(index, 4), lax.rem(index, 4))

    barrier = pltpu.get_barrier_semaphore()

    @pl.loop(1, ROWS)
    def _(step):
        pl.semaphore_signal(
            barrier, inc=1, device_id=in_rows(lax.rem(row + step, ROWS)), device_id_type=MESH
        )

    @pl.loop(1, RING)
    def _(step):
        pl.semaphore_signal(
            barrier, inc=1, device_id=in_ring(lax.rem(ring + step, RING)), device_id_type=MESH
        )

    tables = [
        pltpu.make_async_copy(source, target, table_sem.at[place])
        for place, (source, target) in enumerate(
            (
                (atom_x_hbm, atom_x),
                (atom_y_hbm, atom_y),
                (atom_z_hbm, atom_z),
                (charges_hbm, charges),
                (table_hbm, table),
                (background_hbm, background),
                (ahead_y_hbm, ahead_y),
                (green_x_hbm, green_x),
                (green_y_hbm, green_y),
                (back_y_hbm, back_y),
            )
        )
    ]
    for copy in tables:
        copy.start()

    for copy in tables[:4]:
        copy.wait()
    slot = lax.broadcasted_iota(jnp.int32, (1, SLOTS), 1)
    live = jnp.where(slot < counts[0, 0], charges[0], 0.0)
    inner_y = lax.broadcasted_iota(jnp.int32, (EY, SLOTS), 0)
    inner_y = jnp.where(inner_y < CY + 2, inner_y, inner_y - EY).astype(F32)
    height_y, slope_y = spline(atom_y[0] - inner_y + 2.5)
    inner_x = lax.broadcasted_iota(jnp.int32, (CX + 8, SLOTS), 0)
    inner_x = jnp.where(inner_x < CX + 2, inner_x, inner_x - CX - 4).astype(F32)
    height_x, slope_x = spline(atom_x[0] - inner_x + 2.5)

    @pl.loop(0, N // 64)
    def _(block):
        first = pl.multiple_of(block * 64, 64)
        plane = (lax.broadcasted_iota(jnp.int32, (64, SLOTS), 0) + first).astype(F32)
        offset = atom_z[0] - plane
        offset = jnp.where(offset >= N / 2.0, offset - N, offset)
        offset = jnp.where(offset < -N / 2.0, offset + N, offset)
        height, slope = spline(offset + 2.5)
        for value, target in ((height, weight_z), (slope, slope_z)):
            high, low = halves(value)
            target[pl.ds(first, 64), :] = high
            target[pl.ds(N + first, 64), :] = high
            target[pl.ds(2 * N + first, 64), :] = low

    charged_y = height_y * live
    for place in range(4):
        mixed[MAIN + place * EY : MAIN + place * EY + EY, :] = (
            height_x[CX + place : CX + place + 1] * charged_y
        )
    high, low = halves(mixed[MAIN:, :])
    for side in range(2):
        rows = slice(side * 32, side * 32 + 32)
        halo_out[side] = (
            dot_nt(high[rows], weight_z[:N, :])
            + dot_nt(high[rows], weight_z[2 * N :, :])
            + dot_nt(low[rows], weight_z[:N, :])
        )

    pl.semaphore_wait(barrier, ROWS - 1 + RING - 1)
    sides = (lax.rem(ring + 1, RING), lax.rem(ring + RING - 1, RING))
    for side in range(2):
        pltpu.make_async_remote_copy(
            halo_out.at[side],
            halo_in.at[side],
            send_halo.at[side],
            recv_halo.at[side],
            device_id=in_ring(sides[side]),
            device_id_type=MESH,
        ).start()

    for y in range(EY):
        for group in range(GROUPS):
            mixed[group * 128 + y * 8 : group * 128 + y * 8 + 8, :] = (
                height_x[group * 8 : group * 8 + 8] * charged_y[y : y + 1]
            )
    high, low = halves(mixed[:MAIN, :])
    mixed_parts[:, :SLOTS] = high
    mixed_parts[:, SLOTS : 2 * SLOTS] = high
    mixed_parts[:, 2 * SLOTS :] = low

    tables[4].wait()
    high, low = halves(dot(table[...], weight_z[...]))
    deposit_parts[:, :SLOTS] = high
    deposit_parts[:, SLOTS : 2 * SLOTS] = low
    deposit_parts[:, 2 * SLOTS :] = high
    for chunk in range(CHUNKS):
        for place, value in enumerate((high, low, high)):
            pull_parts[chunk, place * 128 : place * 128 + 128, :SLOTS] = value[
                chunk * 128 : chunk * 128 + 128
            ]
    spread_tiles = spread_out.reshape(CHUNKS, GROUPS, 128, 128)

    @pl.loop(0, CHUNKS)
    def _(chunk):
        first = pl.multiple_of(chunk * 128, 128)
        atoms = dot_nt(deposit_parts[pl.ds(first, 128), :], mixed_parts[...])
        for group in range(GROUPS):
            spread_tiles[chunk, group] = atoms[:, group * 128 : group * 128 + 128]

    tables[5].wait()
    for tile in range(3):
        lanes = slice(tile * 128, tile * 128 + 128)
        for group in range(GROUPS):
            for y in range(CY):
                charge[tile, group * 128 + y * 8 : group * 128 + y * 8 + 8, :] = background[
                    y, group * 8 : group * 8 + 8, lanes
                ]
            charge[tile, group * 128 + CY * 8 : group * 128 + 128, :] = jnp.zeros(
                (128 - CY * 8, 128), F32
            )
    for side, first in ((0, 0), (1, 2 * 128 + 6)):
        pltpu.make_async_copy(halo_in.at[side], halo_in.at[side], recv_halo.at[side]).wait()
        for place in range(2):
            rows = pl.ds(first + place, EY, 8)
            for tile in range(3):
                lanes = slice(tile * 128, tile * 128 + 128)
                charge[tile, rows, :] += halo_in[side, place * EY : place * EY + EY, lanes]
    for tile in range(3):
        high, low = halves(charge[tile])
        for place, value in enumerate((high, high, low)):
            charge_parts[:, place * N + tile * 128 : place * N + tile * 128 + 128] = value

    @pl.loop(0, CHUNKS)
    def _(chunk):
        first = pl.multiple_of(chunk * 128, 128)
        waves = dot_nt(table[pl.ds(first, 128), :], charge_parts[...])
        for group in range(GROUPS):
            spread_tiles[chunk, group] += waves[:, group * 128 : group * 128 + 128]
        pltpu.make_async_copy(
            spread_out.at[chunk, :, row], spread_in.at[chunk, :, :, row], recv_one.at[chunk]
        ).start()

        @pl.loop(1, ROWS)
        def _(step):
            target = lax.rem(row + step, ROWS)
            pltpu.make_async_remote_copy(
                spread_out.at[chunk, :, target],
                spread_in.at[chunk, :, :, row],
                send_one.at[chunk],
                recv_one.at[chunk],
                device_id=in_rows(target),
                device_id_type=MESH,
            ).start()

    high, low = halves(dot(table[...], slope_z[...]))
    for chunk in range(CHUNKS):
        for place, value in enumerate((high, low, high)):
            pull_parts[chunk, place * 128 : place * 128 + 128, SLOTS:] = value[
                chunk * 128 : chunk * 128 + 128
            ]

    tables[6].wait()
    spread_got = spread_in.reshape(CHUNKS, GROUPS, 128, 128)

    @pl.loop(0, CHUNKS)
    def _(chunk):
        pltpu.make_async_copy(spread_in.at[chunk], spread_in.at[chunk], recv_one.at[chunk]).wait()
        for group in range(GROUPS):
            flipped = spread_got[chunk, group].T
            for quarter in range(4):
                items = [flipped[(quarter * 4 + j) * 8 : (quarter * 4 + j) * 8 + 8] for j in range(4)]
                for k, item in enumerate(exchange_blocks(items)):
                    lines[
                        k * CX + group * 8 : k * CX + group * 8 + 8,
                        quarter * 128 : quarter * 128 + 128,
                    ] = item
        high, low = halves(lines[...])
        waves = dot(jnp.concatenate([high, high, low], axis=1), ahead_y[...])
        for k in range(4):
            for tile in range(3):
                wave_out[chunk * 12 + k * 3 + tile] = waves[
                    k * CX : k * CX + CX, tile * 128 : tile * 128 + 128
                ]

        @pl.loop(0, 12)
        def _(step):
            unit = chunk * 12 + lax.rem(step + lax.div(3 * ring, 4), 12)
            target = lax.rem(5 * unit + 8 * core, RING)
            place = lax.div(unit, RING)

            @pl.when(target != ring)
            def _():
                pltpu.make_async_remote_copy(
                    wave_out.at[unit],
                    wave_in.at[place, ring],
                    send_two.at[unit],
                    recv_two.at[place],
                    device_id=in_ring(target),
                    device_id_type=MESH,
                ).start()

            @pl.when(target == ring)
            def _():
                pltpu.make_async_copy(
                    wave_out.at[unit], wave_in.at[place, ring], recv_two.at[place]
                ).start()

    for copy in tables[7:9]:
        copy.wait()
    base = lax.rem(13 * (ring + RING - 8 * core), RING)
    n_places = lax.div(UNITS - 1 - base, RING) + 1

    @pl.loop(0, n_places)
    def _(place):
        unit = place * RING + base
        pltpu.make_async_copy(
            wave_in.at[place, :], wave_in.at[place, :], recv_two.at[place]
        ).wait()
        high, low = halves(wave_in[place].reshape(N, 128))
        waves = dot(table[...], jnp.concatenate([high, high, low], axis=0))
        within = lax.rem(unit, 12)
        wave_z = lax.div(unit, 12) * 128 + row * 4 + lax.div(within, 3)
        tile = lax.rem(within, 3)
        decay = green_x[0, pl.ds(wave_z, 1), :] * green_y[0, tile]
        square = green_x[1, pl.ds(wave_z, 1), :] + green_y[1, tile]
        squares = green_x[1].reshape(N // 8, 8, 128) + square[None]
        decays = green_x[0].reshape(N // 8, 8, 128) * decay[None]
        green = jnp.where(squares > 0.0, decays / jnp.where(squares > 0.0, squares, 1.0), 0.0)
        high, low = halves(waves * green.reshape(N, 128))
        cells = dot(table[...], jnp.concatenate([high, high, low], axis=0))
        back_out[place] = cells.reshape(RING, CX, 128)
        group = lax.div(unit, 12)
        pltpu.make_async_copy(
            back_out.at[place, ring], back_in.at[unit], recv_three.at[group]
        ).start()

        @pl.loop(1, RING)
        def _(step):
            target = lax.rem(ring + step, RING)
            pltpu.make_async_remote_copy(
                back_out.at[place, target],
                back_in.at[unit],
                send_three.at[place, target],
                recv_three.at[group],
                device_id=in_ring(target),
                device_id_type=MESH,
            ).start()

    tables[9].wait()
    cell_tiles = cell_out.reshape(CHUNKS, GROUPS, 128, 128)

    @pl.loop(0, CHUNKS)
    def _(chunk):
        units = pl.ds(chunk * 12, 12)
        pltpu.make_async_copy(
            back_in.at[units], back_in.at[units], recv_three.at[chunk]
        ).wait()
        tiles = [
            jnp.concatenate([back_in[chunk * 12 + k * 3 + tile] for tile in range(3)], axis=1)
            for k in range(4)
        ]
        high, low = halves(jnp.concatenate(tiles, axis=0))
        lines[...] = dot(jnp.concatenate([high, high, low], axis=1), back_y[...])
        for group in range(GROUPS):
            for quarter in range(4):
                items = [
                    lines[
                        k * CX + group * 8 : k * CX + group * 8 + 8,
                        quarter * 128 : quarter * 128 + 128,
                    ]
                    for k in range(4)
                ]
                for j, item in enumerate(exchange_blocks(items)):
                    turned[(quarter * 4 + j) * 8 : (quarter * 4 + j) * 8 + 8, :] = item
            cell_tiles[chunk, group] = turned[...].T
        pltpu.make_async_copy(
            cell_out.at[chunk, :, :, row], cell_in.at[chunk, :, row], recv_four.at[chunk]
        ).start()

        @pl.loop(1, ROWS)
        def _(step):
            target = lax.rem(row + step, ROWS)
            pltpu.make_async_remote_copy(
                cell_out.at[chunk, :, :, target],
                cell_in.at[chunk, :, row],
                send_four.at[chunk],
                recv_four.at[chunk],
                device_id=in_rows(target),
                device_id_type=MESH,
            ).start()

    cell_got = cell_in.reshape(CHUNKS, GROUPS, 128, 128)
    gathered[...] = jnp.zeros((MAIN + EDGE, 2 * SLOTS), F32)

    @pl.loop(0, CHUNKS)
    def _(chunk):
        pltpu.make_async_copy(cell_in.at[chunk], cell_in.at[chunk], recv_four.at[chunk]).wait()
        for group in range(GROUPS):
            cells[group * 128 : group * 128 + 128, :] = cell_got[chunk, group].T
        for side, first in ((0, 2 * 128 + 6), (1, 0)):
            for place in range(2):
                flank_out[chunk, side, place * EY : place * EY + EY, :] = cells[
                    pl.ds(first + place, EY, 8), :
                ]
            pltpu.make_async_remote_copy(
                flank_out.at[chunk, side],
                flank_in.at[chunk, side],
                send_flank.at[chunk, side],
                recv_flank.at[chunk, side],
                device_id=in_ring(sides[side]),
                device_id_type=MESH,
            ).start()
        high, low = halves(cells[...])
        gathered[:MAIN, :] += dot(jnp.concatenate([high, high, low], axis=1), pull_parts[chunk])

    @pl.loop(0, CHUNKS)
    def _(chunk):
        for side in range(2):
            pltpu.make_async_copy(
                flank_in.at[chunk, side], flank_in.at[chunk, side], recv_flank.at[chunk, side]
            ).wait()
        high, low = halves(flank_in[chunk].reshape(EDGE, 128))
        gathered[MAIN:, :] += dot(jnp.concatenate([high, high, low], axis=1), pull_parts[chunk])

    force_x = jnp.zeros((8, SLOTS), F32)
    force_y = jnp.zeros((8, SLOTS), F32)
    force_z = jnp.zeros((8, SLOTS), F32)
    for y in range(EY):
        along_x = jnp.zeros((8, SLOTS), F32)
        turned_x = jnp.zeros((8, SLOTS), F32)
        depth_x = jnp.zeros((8, SLOTS), F32)
        for group in range(GROUPS):
            first = group * 128 + y * 8
            plain = gathered[first : first + 8, :SLOTS]
            deriv = gathered[first : first + 8, SLOTS:]
            weight = height_x[group * 8 : group * 8 + 8]
            along_x += weight * plain
            turned_x += slope_x[group * 8 : group * 8 + 8] * plain
            depth_x += weight * deriv
        force_x += height_y[y : y + 1] * turned_x
        force_y += slope_y[y : y + 1] * along_x
        force_z += height_y[y : y + 1] * depth_x
    for half in range(2):
        along_x = jnp.zeros((8, SLOTS), F32)
        turned_x = jnp.zeros((8, SLOTS), F32)
        depth_x = jnp.zeros((8, SLOTS), F32)
        for place, x in enumerate((CX + 2, CX + 3, CX, CX + 1)):
            first = MAIN + place * EY + half * 8
            plain = gathered[first : first + 8, :SLOTS]
            deriv = gathered[first : first + 8, SLOTS:]
            along_x += height_x[x : x + 1] * plain
            turned_x += slope_x[x : x + 1] * plain
            depth_x += height_x[x : x + 1] * deriv
        height = height_y[half * 8 : half * 8 + 8]
        force_x += height * turned_x
        force_y += slope_y[half * 8 : half * 8 + 8] * along_x
        force_z += height * depth_x
    for place, force in enumerate((force_x, force_y, force_z)):
        out[place, 0] = -live * jnp.sum(force, axis=0, keepdims=True)

    for side in range(2):
        pltpu.make_async_copy(halo_out.at[side], halo_out.at[side], send_halo.at[side]).wait()

    @pl.loop(0, CHUNKS)
    def _(chunk):
        sizes = spread_out.at[chunk, :, 0 : ROWS - 1]
        pltpu.make_async_copy(sizes, sizes, send_one.at[chunk]).wait()
        sizes = cell_in.at[chunk, :, 0 : ROWS - 1]
        pltpu.make_async_copy(sizes, sizes, send_four.at[chunk]).wait()
        for side in range(2):
            sizes = flank_out.at[chunk, side]
            pltpu.make_async_copy(sizes, sizes, send_flank.at[chunk, side]).wait()

    @pl.loop(0, UNITS)
    def _(unit):
        @pl.when(lax.rem(5 * unit + 8 * core, RING) != ring)
        def _():
            sizes = wave_out.at[unit]
            pltpu.make_async_copy(sizes, sizes, send_two.at[unit]).wait()

    @pl.loop(0, n_places)
    def _(place):
        @pl.loop(1, RING)
        def _(step):
            target = lax.rem(ring + step, RING)
            sizes = back_out.at[place, target]
            pltpu.make_async_copy(sizes, sizes, send_three.at[place, target]).wait()


def solution(mesh):
    tables = make_tables()

    def per_device(*args):
        vmem = pl.BlockSpec(memory_space=pltpu.VMEM)
        anywhere = pl.BlockSpec(memory_space=pl.ANY)
        held = [pltpu.VMEM(value.shape, value.dtype) for value in (*args[:4], args[5], *tables)]
        return pl.pallas_call(
            kernel,
            out_shape=jax.ShapeDtypeStruct((3, 1, 1, SLOTS), F32),
            in_specs=[anywhere] * 4 + [pl.BlockSpec(memory_space=pltpu.SMEM)] + [anywhere] * 6,
            out_specs=vmem,
            scratch_shapes=held
            + [
                pltpu.SemaphoreType.DMA((10,)),
                pltpu.VMEM((3 * N, SLOTS), BF16),
                pltpu.VMEM((3 * N, SLOTS), BF16),
                pltpu.VMEM((MAIN + EDGE, SLOTS), F32),
                pltpu.VMEM((MAIN, 3 * SLOTS), BF16),
                pltpu.VMEM((3, MAIN, 128), F32),
                pltpu.VMEM((MAIN, 3 * N), BF16),
                pltpu.VMEM((N, 3 * SLOTS), BF16),
                pltpu.VMEM((CHUNKS, 3 * 128, 2 * SLOTS), BF16),
                pltpu.VMEM((4 * CX, EY * ROWS), F32),
                pltpu.VMEM((128, 128), F32),
                pltpu.VMEM((CHUNKS, GROUPS, ROWS, 4, 1, 128), F32),
                pltpu.VMEM((CHUNKS, GROUPS, 4, ROWS, 1, 128), F32),
                pltpu.VMEM((UNITS, CX, 128), F32),
                pltpu.VMEM((3, RING, CX, 128), F32),
                pltpu.VMEM((3, RING, CX, 128), F32),
                pltpu.VMEM((UNITS, CX, 128), F32),
                pltpu.VMEM((CHUNKS, GROUPS, 4, ROWS, 1, 128), F32),
                pltpu.VMEM((CHUNKS, GROUPS, ROWS, 4, 1, 128), F32),
                pltpu.VMEM((2, 32, N), F32),
                pltpu.VMEM((2, 32, N), F32),
                pltpu.VMEM((CHUNKS, 2, 32, 128), F32),
                pltpu.VMEM((CHUNKS, 2, 32, 128), F32),
                pltpu.VMEM((MAIN, 128), F32),
                pltpu.VMEM((MAIN + EDGE, 2 * SLOTS), F32),
                pltpu.SemaphoreType.DMA((CHUNKS,)),
                pltpu.SemaphoreType.DMA((CHUNKS,)),
                pltpu.SemaphoreType.DMA((UNITS,)),
                pltpu.SemaphoreType.DMA((3,)),
                pltpu.SemaphoreType.DMA((3, RING)),
                pltpu.SemaphoreType.DMA((CHUNKS,)),
                pltpu.SemaphoreType.DMA((CHUNKS,)),
                pltpu.SemaphoreType.DMA((CHUNKS,)),
                pltpu.SemaphoreType.DMA((2,)),
                pltpu.SemaphoreType.DMA((2,)),
                pltpu.SemaphoreType.DMA((CHUNKS, 2)),
                pltpu.SemaphoreType.DMA((CHUNKS, 2)),
            ],
            compiler_params=pltpu.CompilerParams(
                collective_id=0, has_side_effects=True, vmem_limit_bytes=60 * 1024 * 1024
            ),
            name="ewald",
        )(*args, *(jnp.asarray(table) for table in tables))

    pencils = P("gx", ("gy", "gz"), None)
    return jax.shard_map(
        per_device,
        mesh=mesh,
        in_specs=(pencils,) * 4 + (P("gx", ("gy", "gz")), P(("gy", "gz"), "gx", None)),
        out_specs=P(None, "gx", ("gy", "gz"), None),
        check_vma=False,
    )
```

```python
import math

import jax
import jax.numpy as jnp
import ml_dtypes
import numpy as np
from jax import lax
from jax.experimental import pallas as pl
from jax.experimental.pallas import tpu as pltpu
from jax.sharding import PartitionSpec as P

COULOMB = 6.5
N = 384
RING = 16
ROWS = 32
CX, CY = N // RING, N // ROWS
EY = 16
GROUPS = CX // 8
MAIN = GROUPS * 128
EDGE = 64
SLOTS = 256
CHUNKS = 3
UNITS = 36
MESH = pl.DeviceIdType.MESH
F32 = jnp.float32
BF16 = jnp.bfloat16


def parts(table):
    high = table.astype(ml_dtypes.bfloat16)
    low = (table - high.astype(np.float64)).astype(ml_dtypes.bfloat16)
    return high, low


def cas(rows, columns):
    angles = (rows[:, None] * columns[None, :] % N) * (2.0 * math.pi / N)
    return np.cos(angles) + np.sin(angles)


def wide_table(table):
    high, low = parts(table)
    return np.concatenate([high, low, high], axis=1)


def tall_table(table):
    high, low = parts(table)
    return np.concatenate([high, low, high], axis=0)


def make_tables():
    wave = np.arange(N)
    along = wide_table(cas(wave, wave))
    inner_y = np.arange(EY)
    inner_y = np.where(inner_y < CY + 2, inner_y, inner_y - EY)
    cell_y = (inner_y[:, None] + CY * np.arange(ROWS)[None, :]).reshape(-1) % N
    ahead_y = tall_table(cas(cell_y, wave))
    back_y = tall_table(cas(wave, cell_y))
    signed = np.where(wave <= N // 2, wave, wave - N) / N
    angles = 2.0 * math.pi / N * wave
    modulus = (230.0 + 152.0 * np.cos(angles) + 2.0 * np.cos(2.0 * angles)) / 384.0
    decay = np.exp(-(math.pi**2) * signed**2) / modulus**2
    factor = COULOMB / (math.pi * N * N * N)
    green_x = np.broadcast_to(np.stack([decay, signed**2])[:, :, None], (2, N, 128))
    green_y = np.stack([decay * factor, signed**2]).reshape(2, 3, 1, 128)
    green_y = np.broadcast_to(green_y, (2, 3, 8, 128))
    return (
        along,
        ahead_y,
        back_y,
        np.ascontiguousarray(green_x, dtype=np.float32),
        np.ascontiguousarray(green_y, dtype=np.float32),
    )


def spline(offset):
    distance = jnp.minimum(offset, 5.0 - offset)
    ramp_zero = jnp.maximum(distance, 0.0)
    ramp_one = jnp.maximum(distance - 1.0, 0.0)
    ramp_two = jnp.maximum(distance - 2.0, 0.0)
    cube_zero = ramp_zero * ramp_zero * ramp_zero
    cube_one = ramp_one * ramp_one * ramp_one
    cube_two = ramp_two * ramp_two * ramp_two
    height = (cube_zero * ramp_zero - 5.0 * cube_one * ramp_one + 10.0 * cube_two * ramp_two) * (
        1.0 / 24.0
    )
    gradient = (cube_zero - 5.0 * cube_one + 10.0 * cube_two) * (1.0 / 6.0)
    return height, jnp.where(offset < 2.5, gradient, -gradient)


def halves(value):
    high = value.astype(BF16)
    return high, (value - high.astype(F32)).astype(BF16)


def dot(left, right):
    return jnp.dot(left, right, preferred_element_type=F32)


def dot_nt(left, right):
    return lax.dot_general(left, right, (((1,), (1,)), ((), ())), preferred_element_type=F32)


def exchange_blocks(items):
    lane = lax.broadcasted_iota(jnp.int32, (8, 128), 1)
    low = lane < 64
    even = (lane // 32) % 2 == 0

    def pair(first, second, shift, mask):
        back = pltpu.roll(second, shift, 1)
        ahead = pltpu.roll(first, 128 - shift, 1)
        return jnp.where(mask, first, back), jnp.where(mask, ahead, second)

    zero, two = pair(items[0], items[2], 64, low)
    one, three = pair(items[1], items[3], 64, low)
    zero, one = pair(zero, one, 32, even)
    two, three = pair(two, three, 32, even)
    return zero, one, two, three


def kernel(
    atom_x_hbm,
    atom_y_hbm,
    atom_z_hbm,
    charges_hbm,
    counts,
    background_hbm,
    table_hbm,
    ahead_y_hbm,
    back_y_hbm,
    green_x_hbm,
    green_y_hbm,
    out,
    atom_x,
    atom_y,
    atom_z,
    charges,
    background,
    table,
    ahead_y,
    back_y,
    green_x,
    green_y,
    table_sem,
    weight_z,
    slope_z,
    mixed,
    mixed_parts,
    charge,
    charge_parts,
    deposit_parts,
    pull_parts,
    lines,
    turned,
    spread_out,
    spread_in,
    wave_out,
    wave_in,
    back_out,
    back_in,
    cell_out,
    cell_in,
    halo_out,
    halo_in,
    flank_out,
    flank_in,
    cells,
    gathered,
    send_one,
    recv_one,
    send_two,
    recv_two,
    send_three,
    recv_three,
    send_four,
    recv_four,
    send_halo,
    recv_halo,
    send_flank,
    recv_flank,
):
    ring = lax.axis_index("gx")
    major, minor = lax.axis_index("gy"), lax.axis_index("gz")
    row = major * 4 + minor
    core = lax.rem(minor, 2)

    def in_ring(index):
        return (index, major, minor)

    def in_rows(index):
        return (ring, lax.div(index, 4), lax.rem(index, 4))

    barrier = pltpu.get_barrier_semaphore()

    @pl.loop(1, ROWS)
    def _(step):
        pl.semaphore_signal(
            barrier, inc=1, device_id=in_rows(lax.rem(row + step, ROWS)), device_id_type=MESH
        )

    @pl.loop(1, RING)
    def _(step):
        pl.semaphore_signal(
            barrier, inc=1, device_id=in_ring(lax.rem(ring + step, RING)), device_id_type=MESH
        )

    tables = [
        pltpu.make_async_copy(source, target, table_sem.at[place])
        for place, (source, target) in enumerate(
            (
                (atom_x_hbm, atom_x),
                (atom_y_hbm, atom_y),
                (atom_z_hbm, atom_z),
                (charges_hbm, charges),
                (table_hbm, table),
                (background_hbm, background),
                (ahead_y_hbm, ahead_y),
                (green_x_hbm, green_x),
                (green_y_hbm, green_y),
                (back_y_hbm, back_y),
            )
        )
    ]
    for copy in tables:
        copy.start()

    for copy in tables[:4]:
        copy.wait()
    slot = lax.broadcasted_iota(jnp.int32, (1, SLOTS), 1)
    live = jnp.where(slot < counts[0, 0], charges[0], 0.0)
    inner_y = lax.broadcasted_iota(jnp.int32, (EY, SLOTS), 0)
    inner_y = jnp.where(inner_y < CY + 2, inner_y, inner_y - EY).astype(F32)
    height_y, slope_y = spline(atom_y[0] - inner_y + 2.5)
    inner_x = lax.broadcasted_iota(jnp.int32, (CX + 8, SLOTS), 0)
    inner_x = jnp.where(inner_x < CX + 2, inner_x, inner_x - CX - 4).astype(F32)
    height_x, slope_x = spline(atom_x[0] - inner_x + 2.5)

    @pl.loop(0, N // 64)
    def _(block):
        first = pl.multiple_of(block * 64, 64)
        plane = (lax.broadcasted_iota(jnp.int32, (64, SLOTS), 0) + first).astype(F32)
        offset = atom_z[0] - plane
        offset = jnp.where(offset >= N / 2.0, offset - N, offset)
        offset = jnp.where(offset < -N / 2.0, offset + N, offset)
        height, slope = spline(offset + 2.5)
        for value, target in ((height, weight_z), (slope, slope_z)):
            high, low = halves(value)
            target[pl.ds(first, 64), :] = high
            target[pl.ds(N + first, 64), :] = high
            target[pl.ds(2 * N + first, 64), :] = low

    charged_y = height_y * live
    for place in range(4):
        mixed[MAIN + place * EY : MAIN + place * EY + EY, :] = (
            height_x[CX + place : CX + place + 1] * charged_y
        )
    high, low = halves(mixed[MAIN:, :])
    for side in range(2):
        rows = slice(side * 32, side * 32 + 32)
        halo_out[side] = (
            dot_nt(high[rows], weight_z[:N, :])
            + dot_nt(high[rows], weight_z[2 * N :, :])
            + dot_nt(low[rows], weight_z[:N, :])
        )

    pl.semaphore_wait(barrier, ROWS - 1 + RING - 1)
    sides = (lax.rem(ring + 1, RING), lax.rem(ring + RING - 1, RING))
    for side in range(2):
        pltpu.make_async_remote_copy(
            halo_out.at[side],
            halo_in.at[side],
            send_halo.at[side],
            recv_halo.at[side],
            device_id=in_ring(sides[side]),
            device_id_type=MESH,
        ).start()

    for y in range(EY):
        for group in range(GROUPS):
            mixed[group * 128 + y * 8 : group * 128 + y * 8 + 8, :] = (
                height_x[group * 8 : group * 8 + 8] * charged_y[y : y + 1]
            )
    high, low = halves(mixed[:MAIN, :])
    mixed_parts[:, :SLOTS] = high
    mixed_parts[:, SLOTS : 2 * SLOTS] = high
    mixed_parts[:, 2 * SLOTS :] = low

    tables[4].wait()
    high, low = halves(dot(table[...], weight_z[...]))
    deposit_parts[:, :SLOTS] = high
    deposit_parts[:, SLOTS : 2 * SLOTS] = low
    deposit_parts[:, 2 * SLOTS :] = high
    for chunk in range(CHUNKS):
        for place, value in enumerate((high, low, high)):
            pull_parts[chunk, place * 128 : place * 128 + 128, :SLOTS] = value[
                chunk * 128 : chunk * 128 + 128
            ]
    spread_tiles = spread_out.reshape(CHUNKS, GROUPS, 128, 128)

    @pl.loop(0, CHUNKS)
    def _(chunk):
        first = pl.multiple_of(chunk * 128, 128)
        atoms = dot_nt(deposit_parts[pl.ds(first, 128), :], mixed_parts[...])
        for group in range(GROUPS):
            spread_tiles[chunk, group] = atoms[:, group * 128 : group * 128 + 128]

    tables[5].wait()
    for tile in range(3):
        lanes = slice(tile * 128, tile * 128 + 128)
        for group in range(GROUPS):
            for y in range(CY):
                charge[tile, group * 128 + y * 8 : group * 128 + y * 8 + 8, :] = background[
                    y, group * 8 : group * 8 + 8, lanes
                ]
            charge[tile, group * 128 + CY * 8 : group * 128 + 128, :] = jnp.zeros(
                (128 - CY * 8, 128), F32
            )
    for side, first in ((0, 0), (1, 2 * 128 + 6)):
        pltpu.make_async_copy(halo_in.at[side], halo_in.at[side], recv_halo.at[side]).wait()
        for place in range(2):
            rows = pl.ds(first + place, EY, 8)
            for tile in range(3):
                lanes = slice(tile * 128, tile * 128 + 128)
                charge[tile, rows, :] += halo_in[side, place * EY : place * EY + EY, lanes]
    for tile in range(3):
        high, low = halves(charge[tile])
        for place, value in enumerate((high, high, low)):
            charge_parts[:, place * N + tile * 128 : place * N + tile * 128 + 128] = value

    def post_lines(chunk):
        pltpu.make_async_copy(
            spread_out.at[chunk, :, row], spread_in.at[chunk, :, :, row], recv_one.at[chunk]
        ).start()

        @pl.loop(1, ROWS)
        def _(step):
            target = lax.rem(row + step, ROWS)
            pltpu.make_async_remote_copy(
                spread_out.at[chunk, :, target],
                spread_in.at[chunk, :, :, row],
                send_one.at[chunk],
                recv_one.at[chunk],
                device_id=in_rows(target),
                device_id_type=MESH,
            ).start()

    def lines_left(chunk):
        sizes = spread_out.at[chunk, :, 0 : ROWS - 1]
        pltpu.make_async_copy(sizes, sizes, send_one.at[chunk]).wait()

    @pl.loop(0, CHUNKS)
    def _(chunk):
        first = pl.multiple_of(chunk * 128, 128)
        waves = dot_nt(table[pl.ds(first, 128), :], charge_parts[...])
        for group in range(GROUPS):
            spread_tiles[chunk, group] += waves[:, group * 128 : group * 128 + 128]

        @pl.when(chunk == 0)
        def _():
            post_lines(0)

    lines_left(0)
    post_lines(1)

    def wave_left(unit):
        @pl.when(lax.rem(5 * unit + 8 * core, RING) != ring)
        def _():
            pltpu.make_async_copy(wave_out.at[unit], wave_out.at[unit], send_two.at[unit]).wait()

    def far_first(step):
        half = lax.div(step, 2)
        return lax.rem(ring + RING // 2 + jnp.where(lax.rem(step, 2) == 1, half, -half), RING)

    def cells_left(place, step):
        target = far_first(step)
        sent = back_out.at[place, target]
        pltpu.make_async_copy(sent, sent, send_three.at[place, target]).wait()

    tables[6].wait()
    spread_got = spread_in.reshape(CHUNKS, GROUPS, 128, 128)

    @pl.loop(0, CHUNKS)
    def _(chunk):
        pltpu.make_async_copy(spread_in.at[chunk], spread_in.at[chunk], recv_one.at[chunk]).wait()
        for group in range(GROUPS):
            flipped = spread_got[chunk, group].T
            for quarter in range(4):
                items = [flipped[(quarter * 4 + j) * 8 : (quarter * 4 + j) * 8 + 8] for j in range(4)]
                for k, item in enumerate(exchange_blocks(items)):
                    lines[
                        k * CX + group * 8 : k * CX + group * 8 + 8,
                        quarter * 128 : quarter * 128 + 128,
                    ] = item
        high, low = halves(lines[...])
        waves = dot(jnp.concatenate([high, high, low], axis=1), ahead_y[...])
        for k in range(4):
            for tile in range(3):
                wave_out[chunk * 12 + k * 3 + tile] = waves[
                    k * CX : k * CX + CX, tile * 128 : tile * 128 + 128
                ]

        @pl.loop(1, RING + 1)
        def _(step):
            target = far_first(step)
            within = lax.rem(13 * (target + RING - 8 * core) + RING * 12 - chunk * 12, RING)
            unit = chunk * 12 + within
            place = lax.div(unit, RING)

            @pl.when((chunk > 0) & (within < 12))
            def _():
                wave_left(unit - 12)

            @pl.when((target != ring) & (within < 12))
            def _():
                pltpu.make_async_remote_copy(
                    wave_out.at[unit],
                    wave_in.at[place, ring],
                    send_two.at[unit],
                    recv_two.at[place],
                    device_id=in_ring(target),
                    device_id_type=MESH,
                ).start()

            @pl.when((target == ring) & (within < 12))
            def _():
                pltpu.make_async_copy(
                    wave_out.at[unit], wave_in.at[place, ring], recv_two.at[place]
                ).start()

        @pl.when(chunk == 0)
        def _():
            lines_left(1)
            post_lines(2)

    high, low = halves(dot(table[...], slope_z[...]))
    for chunk in range(CHUNKS):
        for place, value in enumerate((high, low, high)):
            pull_parts[chunk, place * 128 : place * 128 + 128, SLOTS:] = value[
                chunk * 128 : chunk * 128 + 128
            ]

    for copy in tables[7:9]:
        copy.wait()
    base = lax.rem(13 * (ring + RING - 8 * core), RING)
    n_places = lax.div(UNITS - 1 - base, RING) + 1

    @pl.loop(0, n_places)
    def _(place):
        unit = place * RING + base
        pltpu.make_async_copy(
            wave_in.at[place, :], wave_in.at[place, :], recv_two.at[place]
        ).wait()
        high, low = halves(wave_in[place].reshape(N, 128))
        waves = dot(table[...], jnp.concatenate([high, high, low], axis=0))
        within = lax.rem(unit, 12)
        wave_z = lax.div(unit, 12) * 128 + row * 4 + lax.div(within, 3)
        tile = lax.rem(within, 3)
        decay = green_x[0, pl.ds(wave_z, 1), :] * green_y[0, tile]
        square = green_x[1, pl.ds(wave_z, 1), :] + green_y[1, tile]
        squares = green_x[1].reshape(N // 8, 8, 128) + square[None]
        decays = green_x[0].reshape(N // 8, 8, 128) * decay[None]
        green = jnp.where(squares > 0.0, decays / jnp.where(squares > 0.0, squares, 1.0), 0.0)
        high, low = halves(waves * green.reshape(N, 128))
        cells = dot(table[...], jnp.concatenate([high, high, low], axis=0))
        back_out[place] = cells.reshape(RING, CX, 128)
        group = lax.div(unit, 12)
        pltpu.make_async_copy(
            back_out.at[place, ring], back_in.at[unit], recv_three.at[group]
        ).start()

        @pl.loop(1, RING)
        def _(step):
            target = far_first(step)

            @pl.when((place == 0) & (step <= 12))
            def _():
                wave_left(24 + lax.rem(step - 1 + lax.div(3 * ring, 4), 12))

            @pl.when(place > 0)
            def _():
                cells_left(place - 1, step)

            pltpu.make_async_remote_copy(
                back_out.at[place, target],
                back_in.at[unit],
                send_three.at[place, target],
                recv_three.at[group],
                device_id=in_ring(target),
                device_id_type=MESH,
            ).start()

    tables[9].wait()
    cell_tiles = cell_out.reshape(CHUNKS, GROUPS, 128, 128)

    @pl.loop(0, CHUNKS)
    def _(chunk):
        units = pl.ds(chunk * 12, 12)
        pltpu.make_async_copy(
            back_in.at[units], back_in.at[units], recv_three.at[chunk]
        ).wait()
        tiles = [
            jnp.concatenate([back_in[chunk * 12 + k * 3 + tile] for tile in range(3)], axis=1)
            for k in range(4)
        ]
        high, low = halves(jnp.concatenate(tiles, axis=0))
        lines[...] = dot(jnp.concatenate([high, high, low], axis=1), back_y[...])
        for group in range(GROUPS):
            for quarter in range(4):
                items = [
                    lines[
                        k * CX + group * 8 : k * CX + group * 8 + 8,
                        quarter * 128 : quarter * 128 + 128,
                    ]
                    for k in range(4)
                ]
                for j, item in enumerate(exchange_blocks(items)):
                    turned[(quarter * 4 + j) * 8 : (quarter * 4 + j) * 8 + 8, :] = item
            cell_tiles[chunk, group] = turned[...].T
        pltpu.make_async_copy(
            cell_out.at[chunk, :, :, row], cell_in.at[chunk, :, row], recv_four.at[chunk]
        ).start()

        @pl.loop(1, ROWS)
        def _(step):
            target = lax.rem(row + step, ROWS)
            pltpu.make_async_remote_copy(
                cell_out.at[chunk, :, :, target],
                cell_in.at[chunk, :, row],
                send_four.at[chunk],
                recv_four.at[chunk],
                device_id=in_rows(target),
                device_id_type=MESH,
            ).start()

    cell_got = cell_in.reshape(CHUNKS, GROUPS, 128, 128)
    gathered[...] = jnp.zeros((MAIN + EDGE, 2 * SLOTS), F32)

    @pl.loop(0, CHUNKS)
    def _(chunk):
        pltpu.make_async_copy(cell_in.at[chunk], cell_in.at[chunk], recv_four.at[chunk]).wait()
        for group in range(GROUPS):
            cells[group * 128 : group * 128 + 128, :] = cell_got[chunk, group].T
        for side, first in ((0, 2 * 128 + 6), (1, 0)):
            for place in range(2):
                flank_out[chunk, side, place * EY : place * EY + EY, :] = cells[
                    pl.ds(first + place, EY, 8), :
                ]
            pltpu.make_async_remote_copy(
                flank_out.at[chunk, side],
                flank_in.at[chunk, side],
                send_flank.at[chunk, side],
                recv_flank.at[chunk, side],
                device_id=in_ring(sides[side]),
                device_id_type=MESH,
            ).start()
        high, low = halves(cells[...])
        gathered[:MAIN, :] += dot(jnp.concatenate([high, high, low], axis=1), pull_parts[chunk])

    force_x = jnp.zeros((8, SLOTS), F32)
    force_y = jnp.zeros((8, SLOTS), F32)
    force_z = jnp.zeros((8, SLOTS), F32)
    for y in range(EY):
        along_x = jnp.zeros((8, SLOTS), F32)
        turned_x = jnp.zeros((8, SLOTS), F32)
        depth_x = jnp.zeros((8, SLOTS), F32)
        for group in range(GROUPS):
            first = group * 128 + y * 8
            plain = gathered[first : first + 8, :SLOTS]
            deriv = gathered[first : first + 8, SLOTS:]
            weight = height_x[group * 8 : group * 8 + 8]
            along_x += weight * plain
            turned_x += slope_x[group * 8 : group * 8 + 8] * plain
            depth_x += weight * deriv
        force_x += height_y[y : y + 1] * turned_x
        force_y += slope_y[y : y + 1] * along_x
        force_z += height_y[y : y + 1] * depth_x
    @pl.loop(0, CHUNKS)
    def _(chunk):
        for side in range(2):
            pltpu.make_async_copy(
                flank_in.at[chunk, side], flank_in.at[chunk, side], recv_flank.at[chunk, side]
            ).wait()
        high, low = halves(flank_in[chunk].reshape(EDGE, 128))
        gathered[MAIN:, :] += dot(jnp.concatenate([high, high, low], axis=1), pull_parts[chunk])

    for half in range(2):
        along_x = jnp.zeros((8, SLOTS), F32)
        turned_x = jnp.zeros((8, SLOTS), F32)
        depth_x = jnp.zeros((8, SLOTS), F32)
        for place, x in enumerate((CX + 2, CX + 3, CX, CX + 1)):
            first = MAIN + place * EY + half * 8
            plain = gathered[first : first + 8, :SLOTS]
            deriv = gathered[first : first + 8, SLOTS:]
            along_x += height_x[x : x + 1] * plain
            turned_x += slope_x[x : x + 1] * plain
            depth_x += height_x[x : x + 1] * deriv
        height = height_y[half * 8 : half * 8 + 8]
        force_x += height * turned_x
        force_y += slope_y[half * 8 : half * 8 + 8] * along_x
        force_z += height * depth_x
    for place, force in enumerate((force_x, force_y, force_z)):
        out[place, 0] = -live * jnp.sum(force, axis=0, keepdims=True)

    lines_left(2)
    for side in range(2):
        pltpu.make_async_copy(halo_out.at[side], halo_out.at[side], send_halo.at[side]).wait()

    @pl.loop(0, CHUNKS)
    def _(chunk):
        sizes = cell_in.at[chunk, :, 0 : ROWS - 1]
        pltpu.make_async_copy(sizes, sizes, send_four.at[chunk]).wait()
        for side in range(2):
            sizes = flank_out.at[chunk, side]
            pltpu.make_async_copy(sizes, sizes, send_flank.at[chunk, side]).wait()

    @pl.loop(1, RING)
    def _(step):
        cells_left(n_places - 1, step)


def solution(mesh):
    tables = make_tables()

    def per_device(*args):
        vmem = pl.BlockSpec(memory_space=pltpu.VMEM)
        anywhere = pl.BlockSpec(memory_space=pl.ANY)
        held = [pltpu.VMEM(value.shape, value.dtype) for value in (*args[:4], args[5], *tables)]
        return pl.pallas_call(
            kernel,
            out_shape=jax.ShapeDtypeStruct((3, 1, 1, SLOTS), F32),
            in_specs=[anywhere] * 4 + [pl.BlockSpec(memory_space=pltpu.SMEM)] + [anywhere] * 6,
            out_specs=vmem,
            scratch_shapes=held
            + [
                pltpu.SemaphoreType.DMA((10,)),
                pltpu.VMEM((3 * N, SLOTS), BF16),
                pltpu.VMEM((3 * N, SLOTS), BF16),
                pltpu.VMEM((MAIN + EDGE, SLOTS), F32),
                pltpu.VMEM((MAIN, 3 * SLOTS), BF16),
                pltpu.VMEM((3, MAIN, 128), F32),
                pltpu.VMEM((MAIN, 3 * N), BF16),
                pltpu.VMEM((N, 3 * SLOTS), BF16),
                pltpu.VMEM((CHUNKS, 3 * 128, 2 * SLOTS), BF16),
                pltpu.VMEM((4 * CX, EY * ROWS), F32),
                pltpu.VMEM((128, 128), F32),
                pltpu.VMEM((CHUNKS, GROUPS, ROWS, 4, 1, 128), F32),
                pltpu.VMEM((CHUNKS, GROUPS, 4, ROWS, 1, 128), F32),
                pltpu.VMEM((UNITS, CX, 128), F32),
                pltpu.VMEM((3, RING, CX, 128), F32),
                pltpu.VMEM((3, RING, CX, 128), F32),
                pltpu.VMEM((UNITS, CX, 128), F32),
                pltpu.VMEM((CHUNKS, GROUPS, 4, ROWS, 1, 128), F32),
                pltpu.VMEM((CHUNKS, GROUPS, ROWS, 4, 1, 128), F32),
                pltpu.VMEM((2, 32, N), F32),
                pltpu.VMEM((2, 32, N), F32),
                pltpu.VMEM((CHUNKS, 2, 32, 128), F32),
                pltpu.VMEM((CHUNKS, 2, 32, 128), F32),
                pltpu.VMEM((MAIN, 128), F32),
                pltpu.VMEM((MAIN + EDGE, 2 * SLOTS), F32),
                pltpu.SemaphoreType.DMA((CHUNKS,)),
                pltpu.SemaphoreType.DMA((CHUNKS,)),
                pltpu.SemaphoreType.DMA((UNITS,)),
                pltpu.SemaphoreType.DMA((3,)),
                pltpu.SemaphoreType.DMA((3, RING)),
                pltpu.SemaphoreType.DMA((CHUNKS,)),
                pltpu.SemaphoreType.DMA((CHUNKS,)),
                pltpu.SemaphoreType.DMA((CHUNKS,)),
                pltpu.SemaphoreType.DMA((2,)),
                pltpu.SemaphoreType.DMA((2,)),
                pltpu.SemaphoreType.DMA((CHUNKS, 2)),
                pltpu.SemaphoreType.DMA((CHUNKS, 2)),
            ],
            compiler_params=pltpu.CompilerParams(
                collective_id=0, has_side_effects=True, vmem_limit_bytes=60 * 1024 * 1024
            ),
            name="ewald",
        )(*args, *(jnp.asarray(table) for table in tables))

    pencils = P("gx", ("gy", "gz"), None)
    return jax.shard_map(
        per_device,
        mesh=mesh,
        in_specs=(pencils,) * 4 + (P("gx", ("gy", "gz")), P(("gy", "gz"), "gx", None)),
        out_specs=P(None, "gx", ("gy", "gz"), None),
        check_vma=False,
    )
```

```python
import math

import jax
import jax.numpy as jnp
import ml_dtypes
import numpy as np
from jax import lax
from jax.experimental import pallas as pl
from jax.experimental.pallas import tpu as pltpu
from jax.sharding import PartitionSpec as P

COULOMB = 6.5
N = 384
RING = 16
ROWS = 32
CX, CY = N // RING, N // ROWS
EY = 16
GROUPS = CX // 8
MAIN = GROUPS * 128
EDGE = 64
SLOTS = 256
CHUNKS = 3
UNITS = 36
MESH = pl.DeviceIdType.MESH
F32 = jnp.float32
BF16 = jnp.bfloat16


def parts(table):
    high = table.astype(ml_dtypes.bfloat16)
    low = (table - high.astype(np.float64)).astype(ml_dtypes.bfloat16)
    return high, low


def cas(rows, columns):
    angles = (rows[:, None] * columns[None, :] % N) * (2.0 * math.pi / N)
    return np.cos(angles) + np.sin(angles)


def wide_table(table):
    high, low = parts(table)
    return np.concatenate([high, low, high], axis=1)


def tall_table(table):
    high, low = parts(table)
    return np.concatenate([high, low, high], axis=0)


def make_tables():
    wave = np.arange(N)
    along = wide_table(cas(wave, wave))
    inner_y = np.arange(EY)
    inner_y = np.where(inner_y < CY + 2, inner_y, inner_y - EY)
    cell_y = (inner_y[:, None] + CY * np.arange(ROWS)[None, :]).reshape(-1) % N
    ahead_y = tall_table(cas(cell_y, wave))
    back_y = tall_table(cas(wave, cell_y))
    signed = np.where(wave <= N // 2, wave, wave - N) / N
    angles = 2.0 * math.pi / N * wave
    modulus = (230.0 + 152.0 * np.cos(angles) + 2.0 * np.cos(2.0 * angles)) / 384.0
    decay = np.exp(-(math.pi**2) * signed**2) / modulus**2
    factor = COULOMB / (math.pi * N * N * N)
    green_x = np.broadcast_to(np.stack([decay, signed**2])[:, :, None], (2, N, 128))
    green_y = np.stack([decay * factor, signed**2]).reshape(2, 3, 1, 128)
    green_y = np.broadcast_to(green_y, (2, 3, 8, 128))
    return (
        along,
        ahead_y,
        back_y,
        np.ascontiguousarray(green_x, dtype=np.float32),
        np.ascontiguousarray(green_y, dtype=np.float32),
    )


def ramps(offset):
    distance = jnp.minimum(offset, 5.0 - offset)
    return (
        jnp.maximum(distance, 0.0),
        jnp.maximum(distance - 1.0, 0.0),
        jnp.maximum(distance - 2.0, 0.0),
    )


def spline(offset):
    zero, one, two = (ramp * ramp for ramp in ramps(offset))
    return (zero * zero - 5.0 * (one * one) + 10.0 * (two * two)) * (1.0 / 24.0)


def spline_slope(offset):
    zero, one, two = (ramp * ramp * ramp for ramp in ramps(offset))
    slope = (zero - 5.0 * one + 10.0 * two) * (1.0 / 6.0)
    return jnp.where(offset < 2.5, slope, -slope)


def halves(value):
    high = value.astype(BF16)
    return high, (value - high.astype(F32)).astype(BF16)


def dot(left, right):
    return jnp.dot(left, right, preferred_element_type=F32)


def dot_nt(left, right):
    return lax.dot_general(left, right, (((1,), (1,)), ((), ())), preferred_element_type=F32)


def exchange_blocks(items):
    lane = lax.broadcasted_iota(jnp.int32, (8, 128), 1)
    low = lane < 64
    even = (lane // 32) % 2 == 0

    def pair(first, second, shift, mask):
        back = pltpu.roll(second, shift, 1)
        ahead = pltpu.roll(first, 128 - shift, 1)
        return jnp.where(mask, first, back), jnp.where(mask, ahead, second)

    zero, two = pair(items[0], items[2], 64, low)
    one, three = pair(items[1], items[3], 64, low)
    zero, one = pair(zero, one, 32, even)
    two, three = pair(two, three, 32, even)
    return zero, one, two, three


def kernel(
    atom_x_hbm,
    atom_y_hbm,
    atom_z_hbm,
    charges_hbm,
    counts,
    background_hbm,
    table_hbm,
    ahead_y_hbm,
    back_y_hbm,
    green_x_hbm,
    green_y_hbm,
    out,
    atom_x,
    atom_y,
    atom_z,
    charges,
    background,
    table,
    ahead_y,
    back_y,
    green_x,
    green_y,
    table_sem,
    weight_z,
    slope_z,
    mixed,
    mixed_parts,
    charge,
    charge_parts,
    pull_parts,
    lines,
    turned,
    spread_out,
    spread_in,
    wave_out,
    wave_in,
    back_out,
    back_in,
    cell_out,
    cell_in,
    halo_out,
    halo_in,
    flank_out,
    flank_in,
    cells,
    gathered,
    send_one,
    recv_one,
    send_two,
    recv_two,
    send_three,
    recv_three,
    send_four,
    recv_four,
    send_halo,
    recv_halo,
    send_flank,
    recv_flank,
):
    ring = lax.axis_index("gx")
    major, minor = lax.axis_index("gy"), lax.axis_index("gz")
    row = major * 4 + minor
    core = lax.rem(minor, 2)

    def in_ring(index):
        return (index, major, minor)

    def in_rows(index):
        return (ring, lax.div(index, 4), lax.rem(index, 4))

    barrier = pltpu.get_barrier_semaphore()

    def far_first(step, size):
        half = lax.div(step, 2)
        return size // 2 + jnp.where(lax.rem(step, 2) == 1, half, -half)

    def ring_target(step):
        return lax.rem(ring + far_first(step, RING), RING)

    chip_x = 2 * lax.div(minor, 2) + lax.div(major, 4)
    chip_y = lax.rem(major, 4)

    def row_target(step):
        x = lax.rem(chip_x + far_first(lax.div(step, 8) + 1, 4), 4)
        y = lax.rem(chip_y + far_first(lax.rem(lax.div(step, 2), 4) + 1, 4), 4)
        other = lax.rem(core + step, 2)
        return (4 * lax.rem(x, 2) + y) * 4 + 2 * lax.div(x, 2) + other

    @pl.loop(1, RING)
    def _(step):
        pl.semaphore_signal(
            barrier, inc=1, device_id=in_ring(ring_target(step)), device_id_type=MESH
        )

    @pl.loop(0, ROWS)
    def _(step):
        @pl.when(step != ROWS - 2)
        def _():
            pl.semaphore_signal(
                barrier, inc=1, device_id=in_rows(row_target(step)), device_id_type=MESH
            )

    tables = [
        pltpu.make_async_copy(source, target, table_sem.at[place])
        for place, (source, target) in enumerate(
            (
                (atom_x_hbm, atom_x),
                (atom_y_hbm, atom_y),
                (atom_z_hbm, atom_z),
                (charges_hbm, charges),
                (table_hbm, table),
                (background_hbm, background),
                (ahead_y_hbm, ahead_y),
                (green_x_hbm, green_x),
                (green_y_hbm, green_y),
                (back_y_hbm, back_y),
            )
        )
    ]
    for copy in tables:
        copy.start()

    for copy in tables[:4]:
        copy.wait()
    slot = lax.broadcasted_iota(jnp.int32, (1, SLOTS), 1)
    live = jnp.where(slot < counts[0, 0], charges[0], 0.0)
    inner_y = lax.broadcasted_iota(jnp.int32, (EY, SLOTS), 0)
    inner_y = jnp.where(inner_y < CY + 2, inner_y, inner_y - EY).astype(F32)
    offset_y = atom_y[0] - inner_y + 2.5
    height_y = spline(offset_y)
    inner_x = lax.broadcasted_iota(jnp.int32, (CX + 8, SLOTS), 0)
    inner_x = jnp.where(inner_x < CX + 2, inner_x, inner_x - CX - 4).astype(F32)
    offset_x = atom_x[0] - inner_x + 2.5
    height_x = spline(offset_x)

    def fill_z(function, target):
        @pl.loop(0, N // 64)
        def _(block):
            first = pl.multiple_of(block * 64, 64)
            plane = (lax.broadcasted_iota(jnp.int32, (64, SLOTS), 0) + first).astype(F32)
            offset = atom_z[0] - plane
            offset = jnp.where(offset >= N / 2.0, offset - N, offset)
            offset = jnp.where(offset < -N / 2.0, offset + N, offset)
            high, low = halves(function(offset + 2.5))
            target[pl.ds(first, 64), :] = high
            target[pl.ds(N + first, 64), :] = high
            target[pl.ds(2 * N + first, 64), :] = low

    fill_z(spline, weight_z)
    charged_y = height_y * live
    for place in range(4):
        mixed[MAIN + place * EY : MAIN + place * EY + EY, :] = (
            height_x[CX + place : CX + place + 1] * charged_y
        )
    high, low = halves(mixed[MAIN:, :])
    for side in range(2):
        rows = slice(side * 32, side * 32 + 32)
        halo_out[side] = (
            dot_nt(high[rows], weight_z[:N, :])
            + dot_nt(high[rows], weight_z[2 * N :, :])
            + dot_nt(low[rows], weight_z[:N, :])
        )

    pl.semaphore_wait(barrier, ROWS - 1 + RING - 1)
    sides = (lax.rem(ring + 1, RING), lax.rem(ring + RING - 1, RING))
    for side in range(2):
        pltpu.make_async_remote_copy(
            halo_out.at[side],
            halo_in.at[side],
            send_halo.at[side],
            recv_halo.at[side],
            device_id=in_ring(sides[side]),
            device_id_type=MESH,
        ).start()

    for y in range(EY):
        for group in range(GROUPS):
            mixed[group * 128 + y * 8 : group * 128 + y * 8 + 8, :] = (
                height_x[group * 8 : group * 8 + 8] * charged_y[y : y + 1]
            )
    high, low = halves(mixed[:MAIN, :])
    mixed_parts[:, :SLOTS] = high
    mixed_parts[:, SLOTS : 2 * SLOTS] = high
    mixed_parts[:, 2 * SLOTS :] = low

    tables[4].wait()
    spread_tiles = spread_out.reshape(CHUNKS, GROUPS, 128, 128)

    def deposit(chunk):
        first = pl.multiple_of(chunk * 128, 128)
        high, low = halves(dot(table[pl.ds(first, 128), :], weight_z[...]))
        for place, value in enumerate((high, low, high)):
            pull_parts[chunk, place * 128 : place * 128 + 128, :SLOTS] = value
        atoms = dot_nt(jnp.concatenate([high, low, high], axis=1), mixed_parts[...])
        for group in range(GROUPS):
            spread_tiles[chunk, group] = atoms[:, group * 128 : group * 128 + 128]

    deposit(0)

    tables[5].wait()
    for tile in range(3):
        lanes = slice(tile * 128, tile * 128 + 128)
        for group in range(GROUPS):
            for y in range(CY):
                charge[tile, group * 128 + y * 8 : group * 128 + y * 8 + 8, :] = background[
                    y, group * 8 : group * 8 + 8, lanes
                ]
            charge[tile, group * 128 + CY * 8 : group * 128 + 128, :] = jnp.zeros(
                (128 - CY * 8, 128), F32
            )
    for side, first in ((0, 0), (1, 2 * 128 + 6)):
        pltpu.make_async_copy(halo_in.at[side], halo_in.at[side], recv_halo.at[side]).wait()
        for place in range(2):
            rows = pl.ds(first + place, EY, 8)
            for tile in range(3):
                lanes = slice(tile * 128, tile * 128 + 128)
                charge[tile, rows, :] += halo_in[side, place * EY : place * EY + EY, lanes]
    for tile in range(3):
        high, low = halves(charge[tile])
        for place, value in enumerate((high, high, low)):
            charge_parts[:, place * N + tile * 128 : place * N + tile * 128 + 128] = value

    def post_lines(chunk):
        pltpu.make_async_copy(
            spread_out.at[chunk, :, row], spread_in.at[chunk, :, :, row], recv_one.at[chunk]
        ).start()

        @pl.loop(0, ROWS)
        def _(step):
            target = row_target(step)

            @pl.when(step != ROWS - 2)
            def _():
                pltpu.make_async_remote_copy(
                    spread_out.at[chunk, :, target],
                    spread_in.at[chunk, :, :, row],
                    send_one.at[chunk],
                    recv_one.at[chunk],
                    device_id=in_rows(target),
                    device_id_type=MESH,
                ).start()

    def lines_left(chunk):
        sizes = spread_out.at[chunk, :, 0 : ROWS - 1]
        pltpu.make_async_copy(sizes, sizes, send_one.at[chunk]).wait()

    def add_frozen(chunk):
        first = pl.multiple_of(chunk * 128, 128)
        waves = dot_nt(table[pl.ds(first, 128), :], charge_parts[...])
        for group in range(GROUPS):
            spread_tiles[chunk, group] += waves[:, group * 128 : group * 128 + 128]

    add_frozen(0)
    post_lines(0)

    @pl.loop(1, CHUNKS)
    def _(chunk):
        deposit(chunk)
        add_frozen(chunk)

    lines_left(0)
    post_lines(1)

    def wave_left(unit):
        @pl.when(lax.rem(5 * unit + 8 * core, RING) != ring)
        def _():
            pltpu.make_async_copy(wave_out.at[unit], wave_out.at[unit], send_two.at[unit]).wait()

    def cells_left(place, step):
        target = ring_target(step)
        sent = back_out.at[place, target]
        pltpu.make_async_copy(sent, sent, send_three.at[place, target]).wait()

    tables[6].wait()
    spread_got = spread_in.reshape(CHUNKS, GROUPS, 128, 128)

    @pl.loop(0, CHUNKS)
    def _(chunk):
        pltpu.make_async_copy(spread_in.at[chunk], spread_in.at[chunk], recv_one.at[chunk]).wait()
        for group in range(GROUPS):
            flipped = spread_got[chunk, group].T
            for quarter in range(4):
                items = [flipped[(quarter * 4 + j) * 8 : (quarter * 4 + j) * 8 + 8] for j in range(4)]
                for k, item in enumerate(exchange_blocks(items)):
                    lines[
                        k * CX + group * 8 : k * CX + group * 8 + 8,
                        quarter * 128 : quarter * 128 + 128,
                    ] = item
        high, low = halves(lines[...])
        waves = dot(jnp.concatenate([high, high, low], axis=1), ahead_y[...])
        for k in range(4):
            for tile in range(3):
                wave_out[chunk * 12 + k * 3 + tile] = waves[
                    k * CX : k * CX + CX, tile * 128 : tile * 128 + 128
                ]

        @pl.loop(1, RING + 1)
        def _(step):
            target = ring_target(step)
            within = lax.rem(13 * (target + RING - 8 * core) + RING * 12 - chunk * 12, RING)
            unit = chunk * 12 + within
            place = lax.div(unit, RING)

            @pl.when((chunk > 0) & (within < 12))
            def _():
                wave_left(unit - 12)

            @pl.when((target != ring) & (within < 12))
            def _():
                pltpu.make_async_remote_copy(
                    wave_out.at[unit],
                    wave_in.at[place, ring],
                    send_two.at[unit],
                    recv_two.at[place],
                    device_id=in_ring(target),
                    device_id_type=MESH,
                ).start()

            @pl.when((target == ring) & (within < 12))
            def _():
                pltpu.make_async_copy(
                    wave_out.at[unit], wave_in.at[place, ring], recv_two.at[place]
                ).start()

        @pl.when(chunk == 0)
        def _():
            lines_left(1)
            post_lines(2)

    slope_y = spline_slope(offset_y)
    slope_x = spline_slope(offset_x)
    fill_z(spline_slope, slope_z)
    high, low = halves(dot(table[...], slope_z[...]))
    for chunk in range(CHUNKS):
        for place, value in enumerate((high, low, high)):
            pull_parts[chunk, place * 128 : place * 128 + 128, SLOTS:] = value[
                chunk * 128 : chunk * 128 + 128
            ]

    for copy in tables[7:9]:
        copy.wait()
    base = lax.rem(13 * (ring + RING - 8 * core), RING)
    n_places = lax.div(UNITS - 1 - base, RING) + 1

    @pl.loop(0, n_places)
    def _(place):
        unit = place * RING + base
        pltpu.make_async_copy(
            wave_in.at[place, :], wave_in.at[place, :], recv_two.at[place]
        ).wait()
        high, low = halves(wave_in[place].reshape(N, 128))
        waves = dot(table[...], jnp.concatenate([high, high, low], axis=0))
        within = lax.rem(unit, 12)
        wave_z = lax.div(unit, 12) * 128 + row * 4 + lax.div(within, 3)
        tile = lax.rem(within, 3)
        decay = green_x[0, pl.ds(wave_z, 1), :] * green_y[0, tile]
        square = green_x[1, pl.ds(wave_z, 1), :] + green_y[1, tile]
        squares = green_x[1].reshape(N // 8, 8, 128) + square[None]
        decays = green_x[0].reshape(N // 8, 8, 128) * decay[None]
        green = jnp.where(squares > 0.0, decays / jnp.where(squares > 0.0, squares, 1.0), 0.0)
        high, low = halves(waves * green.reshape(N, 128))
        cells = dot(table[...], jnp.concatenate([high, high, low], axis=0))
        back_out[place] = cells.reshape(RING, CX, 128)
        group = lax.div(unit, 12)
        pltpu.make_async_copy(
            back_out.at[place, ring], back_in.at[unit], recv_three.at[group]
        ).start()

        @pl.loop(1, RING)
        def _(step):
            target = ring_target(step)

            @pl.when((place == 0) & (step <= 12))
            def _():
                wave_left(24 + lax.rem(step - 1 + lax.div(3 * ring, 4), 12))

            @pl.when(place > 0)
            def _():
                cells_left(place - 1, step)

            pltpu.make_async_remote_copy(
                back_out.at[place, target],
                back_in.at[unit],
                send_three.at[place, target],
                recv_three.at[group],
                device_id=in_ring(target),
                device_id_type=MESH,
            ).start()

    tables[9].wait()
    cell_tiles = cell_out.reshape(CHUNKS, GROUPS, 128, 128)

    @pl.loop(0, CHUNKS)
    def _(chunk):
        units = pl.ds(chunk * 12, 12)
        pltpu.make_async_copy(
            back_in.at[units], back_in.at[units], recv_three.at[chunk]
        ).wait()
        tiles = [
            jnp.concatenate([back_in[chunk * 12 + k * 3 + tile] for tile in range(3)], axis=1)
            for k in range(4)
        ]
        high, low = halves(jnp.concatenate(tiles, axis=0))
        lines[...] = dot(jnp.concatenate([high, high, low], axis=1), back_y[...])
        for group in range(GROUPS):
            for quarter in range(4):
                items = [
                    lines[
                        k * CX + group * 8 : k * CX + group * 8 + 8,
                        quarter * 128 : quarter * 128 + 128,
                    ]
                    for k in range(4)
                ]
                for j, item in enumerate(exchange_blocks(items)):
                    turned[(quarter * 4 + j) * 8 : (quarter * 4 + j) * 8 + 8, :] = item
            cell_tiles[chunk, group] = turned[...].T
        pltpu.make_async_copy(
            cell_out.at[chunk, :, :, row], cell_in.at[chunk, :, row], recv_four.at[chunk]
        ).start()

        @pl.loop(0, ROWS)
        def _(step):
            target = row_target(step)

            @pl.when(step != ROWS - 2)
            def _():
                pltpu.make_async_remote_copy(
                    cell_out.at[chunk, :, :, target],
                    cell_in.at[chunk, :, row],
                    send_four.at[chunk],
                    recv_four.at[chunk],
                    device_id=in_rows(target),
                    device_id_type=MESH,
                ).start()

    cell_got = cell_in.reshape(CHUNKS, GROUPS, 128, 128)
    gathered[...] = jnp.zeros((MAIN + EDGE, 2 * SLOTS), F32)

    @pl.loop(0, CHUNKS)
    def _(chunk):
        pltpu.make_async_copy(cell_in.at[chunk], cell_in.at[chunk], recv_four.at[chunk]).wait()
        for group in range(GROUPS):
            cells[group * 128 : group * 128 + 128, :] = cell_got[chunk, group].T
        for side, first in ((0, 2 * 128 + 6), (1, 0)):
            for place in range(2):
                flank_out[chunk, side, place * EY : place * EY + EY, :] = cells[
                    pl.ds(first + place, EY, 8), :
                ]
            pltpu.make_async_remote_copy(
                flank_out.at[chunk, side],
                flank_in.at[chunk, side],
                send_flank.at[chunk, side],
                recv_flank.at[chunk, side],
                device_id=in_ring(sides[side]),
                device_id_type=MESH,
            ).start()
        high, low = halves(cells[...])
        gathered[:MAIN, :] += dot(jnp.concatenate([high, high, low], axis=1), pull_parts[chunk])

    force_x = jnp.zeros((8, SLOTS), F32)
    force_y = jnp.zeros((8, SLOTS), F32)
    force_z = jnp.zeros((8, SLOTS), F32)
    for y in range(EY):
        along_x = jnp.zeros((8, SLOTS), F32)
        turned_x = jnp.zeros((8, SLOTS), F32)
        depth_x = jnp.zeros((8, SLOTS), F32)
        for group in range(GROUPS):
            first = group * 128 + y * 8
            plain = gathered[first : first + 8, :SLOTS]
            deriv = gathered[first : first + 8, SLOTS:]
            weight = height_x[group * 8 : group * 8 + 8]
            along_x += weight * plain
            turned_x += slope_x[group * 8 : group * 8 + 8] * plain
            depth_x += weight * deriv
        force_x += height_y[y : y + 1] * turned_x
        force_y += slope_y[y : y + 1] * along_x
        force_z += height_y[y : y + 1] * depth_x
    @pl.loop(0, CHUNKS)
    def _(chunk):
        for side in range(2):
            pltpu.make_async_copy(
                flank_in.at[chunk, side], flank_in.at[chunk, side], recv_flank.at[chunk, side]
            ).wait()
        high, low = halves(flank_in[chunk].reshape(EDGE, 128))
        gathered[MAIN:, :] += dot(jnp.concatenate([high, high, low], axis=1), pull_parts[chunk])

    for half in range(2):
        along_x = jnp.zeros((8, SLOTS), F32)
        turned_x = jnp.zeros((8, SLOTS), F32)
        depth_x = jnp.zeros((8, SLOTS), F32)
        for place, x in enumerate((CX + 2, CX + 3, CX, CX + 1)):
            first = MAIN + place * EY + half * 8
            plain = gathered[first : first + 8, :SLOTS]
            deriv = gathered[first : first + 8, SLOTS:]
            along_x += height_x[x : x + 1] * plain
            turned_x += slope_x[x : x + 1] * plain
            depth_x += height_x[x : x + 1] * deriv
        height = height_y[half * 8 : half * 8 + 8]
        force_x += height * turned_x
        force_y += slope_y[half * 8 : half * 8 + 8] * along_x
        force_z += height * depth_x
    for place, force in enumerate((force_x, force_y, force_z)):
        out[place, 0] = -live * jnp.sum(force, axis=0, keepdims=True)

    lines_left(2)
    for side in range(2):
        pltpu.make_async_copy(halo_out.at[side], halo_out.at[side], send_halo.at[side]).wait()

    @pl.loop(0, CHUNKS)
    def _(chunk):
        sizes = cell_in.at[chunk, :, 0 : ROWS - 1]
        pltpu.make_async_copy(sizes, sizes, send_four.at[chunk]).wait()
        for side in range(2):
            sizes = flank_out.at[chunk, side]
            pltpu.make_async_copy(sizes, sizes, send_flank.at[chunk, side]).wait()

    @pl.loop(1, RING)
    def _(step):
        cells_left(n_places - 1, step)


def solution(mesh):
    tables = make_tables()

    def per_device(*args):
        vmem = pl.BlockSpec(memory_space=pltpu.VMEM)
        anywhere = pl.BlockSpec(memory_space=pl.ANY)
        held = [pltpu.VMEM(value.shape, value.dtype) for value in (*args[:4], args[5], *tables)]
        return pl.pallas_call(
            kernel,
            out_shape=jax.ShapeDtypeStruct((3, 1, 1, SLOTS), F32),
            in_specs=[anywhere] * 4 + [pl.BlockSpec(memory_space=pltpu.SMEM)] + [anywhere] * 6,
            out_specs=vmem,
            scratch_shapes=held
            + [
                pltpu.SemaphoreType.DMA((10,)),
                pltpu.VMEM((3 * N, SLOTS), BF16),
                pltpu.VMEM((3 * N, SLOTS), BF16),
                pltpu.VMEM((MAIN + EDGE, SLOTS), F32),
                pltpu.VMEM((MAIN, 3 * SLOTS), BF16),
                pltpu.VMEM((3, MAIN, 128), F32),
                pltpu.VMEM((MAIN, 3 * N), BF16),
                pltpu.VMEM((CHUNKS, 3 * 128, 2 * SLOTS), BF16),
                pltpu.VMEM((4 * CX, EY * ROWS), F32),
                pltpu.VMEM((128, 128), F32),
                pltpu.VMEM((CHUNKS, GROUPS, ROWS, 4, 1, 128), F32),
                pltpu.VMEM((CHUNKS, GROUPS, 4, ROWS, 1, 128), F32),
                pltpu.VMEM((UNITS, CX, 128), F32),
                pltpu.VMEM((3, RING, CX, 128), F32),
                pltpu.VMEM((3, RING, CX, 128), F32),
                pltpu.VMEM((UNITS, CX, 128), F32),
                pltpu.VMEM((CHUNKS, GROUPS, 4, ROWS, 1, 128), F32),
                pltpu.VMEM((CHUNKS, GROUPS, ROWS, 4, 1, 128), F32),
                pltpu.VMEM((2, 32, N), F32),
                pltpu.VMEM((2, 32, N), F32),
                pltpu.VMEM((CHUNKS, 2, 32, 128), F32),
                pltpu.VMEM((CHUNKS, 2, 32, 128), F32),
                pltpu.VMEM((MAIN, 128), F32),
                pltpu.VMEM((MAIN + EDGE, 2 * SLOTS), F32),
                pltpu.SemaphoreType.DMA((CHUNKS,)),
                pltpu.SemaphoreType.DMA((CHUNKS,)),
                pltpu.SemaphoreType.DMA((UNITS,)),
                pltpu.SemaphoreType.DMA((3,)),
                pltpu.SemaphoreType.DMA((3, RING)),
                pltpu.SemaphoreType.DMA((CHUNKS,)),
                pltpu.SemaphoreType.DMA((CHUNKS,)),
                pltpu.SemaphoreType.DMA((CHUNKS,)),
                pltpu.SemaphoreType.DMA((2,)),
                pltpu.SemaphoreType.DMA((2,)),
                pltpu.SemaphoreType.DMA((CHUNKS, 2)),
                pltpu.SemaphoreType.DMA((CHUNKS, 2)),
            ],
            compiler_params=pltpu.CompilerParams(
                collective_id=0, has_side_effects=True, vmem_limit_bytes=60 * 1024 * 1024
            ),
            name="ewald",
        )(*args, *(jnp.asarray(table) for table in tables))

    pencils = P("gx", ("gy", "gz"), None)
    return jax.shard_map(
        per_device,
        mesh=mesh,
        in_specs=(pencils,) * 4 + (P("gx", ("gy", "gz")), P(("gy", "gz"), "gx", None)),
        out_specs=P(None, "gx", ("gy", "gz"), None),
        check_vma=False,
    )
```

```python
import math

import jax
import jax.numpy as jnp
import ml_dtypes
import numpy as np
from jax import lax
from jax.experimental import pallas as pl
from jax.experimental.pallas import tpu as pltpu
from jax.sharding import PartitionSpec as P

COULOMB = 6.5
N = 384
RING = 16
ROWS = 32
CX, CY = N // RING, N // ROWS
EY = 16
GROUPS = CX // 8
MAIN = GROUPS * 128
EDGE = 64
SLOTS = 256
CHUNKS = 3
UNITS = 36
MESH = pl.DeviceIdType.MESH
F32 = jnp.float32
BF16 = jnp.bfloat16


def parts(table):
    high = table.astype(ml_dtypes.bfloat16)
    low = (table - high.astype(np.float64)).astype(ml_dtypes.bfloat16)
    return high, low


def cas(rows, columns):
    angles = (rows[:, None] * columns[None, :] % N) * (2.0 * math.pi / N)
    return np.cos(angles) + np.sin(angles)


def wide_table(table):
    high, low = parts(table)
    return np.concatenate([high, low, high], axis=1)


def tall_table(table):
    high, low = parts(table)
    return np.concatenate([high, low, high], axis=0)


def make_tables():
    wave = np.arange(N)
    along = wide_table(cas(wave, wave))
    inner_y = np.arange(EY)
    inner_y = np.where(inner_y < CY + 2, inner_y, inner_y - EY)
    cell_y = (inner_y[:, None] + CY * np.arange(ROWS)[None, :]).reshape(-1) % N
    ahead_y = tall_table(cas(cell_y, wave))
    back_y = tall_table(cas(wave, cell_y))
    signed = np.where(wave <= N // 2, wave, wave - N) / N
    angles = 2.0 * math.pi / N * wave
    modulus = (230.0 + 152.0 * np.cos(angles) + 2.0 * np.cos(2.0 * angles)) / 384.0
    decay = np.exp(-(math.pi**2) * signed**2) / modulus**2
    factor = COULOMB / (math.pi * N * N * N)
    green_x = np.broadcast_to(np.stack([decay, signed**2])[:, :, None], (2, N, 128))
    green_y = np.stack([decay * factor, signed**2]).reshape(2, 3, 1, 128)
    green_y = np.broadcast_to(green_y, (2, 3, 8, 128))
    return (
        along,
        ahead_y,
        back_y,
        np.ascontiguousarray(green_x, dtype=np.float32),
        np.ascontiguousarray(green_y, dtype=np.float32),
    )


def ramps(offset):
    distance = jnp.minimum(offset, 5.0 - offset)
    return (
        jnp.maximum(distance, 0.0),
        jnp.maximum(distance - 1.0, 0.0),
        jnp.maximum(distance - 2.0, 0.0),
    )


def spline(offset):
    zero, one, two = (ramp * ramp for ramp in ramps(offset))
    return (zero * zero - 5.0 * (one * one) + 10.0 * (two * two)) * (1.0 / 24.0)


def spline_slope(offset):
    zero, one, two = (ramp * ramp * ramp for ramp in ramps(offset))
    slope = (zero - 5.0 * one + 10.0 * two) * (1.0 / 6.0)
    return jnp.where(offset < 2.5, slope, -slope)


def halves(value):
    high = value.astype(BF16)
    return high, (value - high.astype(F32)).astype(BF16)


def dot(left, right):
    return jnp.dot(left, right, preferred_element_type=F32)


def dot_nt(left, right):
    return lax.dot_general(left, right, (((1,), (1,)), ((), ())), preferred_element_type=F32)


def exchange_blocks(items):
    lane = lax.broadcasted_iota(jnp.int32, (8, 128), 1)
    low = lane < 64
    even = (lane // 32) % 2 == 0

    def pair(first, second, shift, mask):
        back = pltpu.roll(second, shift, 1)
        ahead = pltpu.roll(first, 128 - shift, 1)
        return jnp.where(mask, first, back), jnp.where(mask, ahead, second)

    zero, two = pair(items[0], items[2], 64, low)
    one, three = pair(items[1], items[3], 64, low)
    zero, one = pair(zero, one, 32, even)
    two, three = pair(two, three, 32, even)
    return zero, one, two, three


def kernel(
    atom_x_hbm,
    atom_y_hbm,
    atom_z_hbm,
    charges_hbm,
    counts,
    background_hbm,
    table_hbm,
    ahead_y_hbm,
    back_y_hbm,
    green_x_hbm,
    green_y_hbm,
    out,
    atom_x,
    atom_y,
    atom_z,
    charges,
    background,
    table,
    ahead_y,
    back_y,
    green_x,
    green_y,
    table_sem,
    weight_z,
    slope_z,
    mixed,
    mixed_parts,
    charge,
    charge_parts,
    pull_parts,
    lines,
    turned,
    spread_out,
    spread_in,
    wave_out,
    wave_in,
    back_out,
    back_in,
    cell_out,
    cell_in,
    halo_out,
    halo_in,
    flank_out,
    flank_in,
    cells,
    gathered,
    send_one,
    recv_one,
    send_two,
    recv_two,
    send_three,
    recv_three,
    send_four,
    recv_four,
    send_halo,
    recv_halo,
    send_flank,
    recv_flank,
):
    ring = lax.axis_index("gx")
    major, minor = lax.axis_index("gy"), lax.axis_index("gz")
    row = major * 4 + minor
    core = lax.rem(minor, 2)

    def in_ring(index):
        return (index, major, minor)

    def in_rows(index):
        return (ring, lax.div(index, 4), lax.rem(index, 4))

    tables = [
        pltpu.make_async_copy(source, target, table_sem.at[place])
        for place, (source, target) in enumerate(
            (
                (atom_x_hbm, atom_x),
                (atom_y_hbm, atom_y),
                (atom_z_hbm, atom_z),
                (charges_hbm, charges),
                (table_hbm, table),
                (background_hbm, background),
                (ahead_y_hbm, ahead_y),
                (green_x_hbm, green_x),
                (green_y_hbm, green_y),
                (back_y_hbm, back_y),
            )
        )
    ]
    for copy in tables[:5]:
        copy.start()

    barrier = pltpu.get_barrier_semaphore()

    def far_first(step, size):
        half = lax.div(step, 2)
        return size // 2 + jnp.where(lax.rem(step, 2) == 1, half, -half)

    def ring_target(step):
        return lax.rem(ring + far_first(step, RING), RING)

    chip_x = 2 * lax.div(minor, 2) + lax.div(major, 4)
    chip_y = lax.rem(major, 4)

    def row_target(step):
        x = lax.rem(chip_x + far_first(lax.div(step, 8) + 1, 4), 4)
        y = lax.rem(chip_y + far_first(lax.rem(lax.div(step, 2), 4) + 1, 4), 4)
        other = lax.rem(core + step, 2)
        return (4 * lax.rem(x, 2) + y) * 4 + 2 * lax.div(x, 2) + other

    @pl.loop(1, RING)
    def _(step):
        pl.semaphore_signal(
            barrier, inc=1, device_id=in_ring(ring_target(step)), device_id_type=MESH
        )

    @pl.loop(0, ROWS)
    def _(step):
        @pl.when(step != ROWS - 2)
        def _():
            pl.semaphore_signal(
                barrier, inc=1, device_id=in_rows(row_target(step)), device_id_type=MESH
            )

    for copy in tables[5:]:
        copy.start()

    for copy in tables[:4]:
        copy.wait()
    slot = lax.broadcasted_iota(jnp.int32, (1, SLOTS), 1)
    live = jnp.where(slot < counts[0, 0], charges[0], 0.0)
    inner_y = lax.broadcasted_iota(jnp.int32, (EY, SLOTS), 0)
    inner_y = jnp.where(inner_y < CY + 2, inner_y, inner_y - EY).astype(F32)
    offset_y = atom_y[0] - inner_y + 2.5
    height_y = spline(offset_y)
    inner_x = lax.broadcasted_iota(jnp.int32, (CX + 8, SLOTS), 0)
    inner_x = jnp.where(inner_x < CX + 2, inner_x, inner_x - CX - 4).astype(F32)
    offset_x = atom_x[0] - inner_x + 2.5
    height_x = spline(offset_x)

    def fill_z(function, target):
        @pl.loop(0, N // 64)
        def _(block):
            first = pl.multiple_of(block * 64, 64)
            plane = (lax.broadcasted_iota(jnp.int32, (64, SLOTS), 0) + first).astype(F32)
            offset = atom_z[0] - plane
            offset = jnp.where(offset >= N / 2.0, offset - N, offset)
            offset = jnp.where(offset < -N / 2.0, offset + N, offset)
            high, low = halves(function(offset + 2.5))
            target[pl.ds(first, 64), :] = high
            target[pl.ds(N + first, 64), :] = high
            target[pl.ds(2 * N + first, 64), :] = low

    fill_z(spline, weight_z)
    charged_y = height_y * live
    for place in range(4):
        mixed[MAIN + place * EY : MAIN + place * EY + EY, :] = (
            height_x[CX + place : CX + place + 1] * charged_y
        )
    high, low = halves(mixed[MAIN:, :])
    edges = (
        dot_nt(high, weight_z[:N, :])
        + dot_nt(high, weight_z[2 * N :, :])
        + dot_nt(low, weight_z[:N, :])
    )
    for side in range(2):
        halo_out[side] = edges[side * 32 : side * 32 + 32]

    pl.semaphore_wait(barrier, ROWS - 1 + RING - 1)
    sides = (lax.rem(ring + 1, RING), lax.rem(ring + RING - 1, RING))
    for side in range(2):
        pltpu.make_async_remote_copy(
            halo_out.at[side],
            halo_in.at[side],
            send_halo.at[side],
            recv_halo.at[side],
            device_id=in_ring(sides[side]),
            device_id_type=MESH,
        ).start()

    for y in range(EY):
        for group in range(GROUPS):
            mixed[group * 128 + y * 8 : group * 128 + y * 8 + 8, :] = (
                height_x[group * 8 : group * 8 + 8] * charged_y[y : y + 1]
            )
    high, low = halves(mixed[:MAIN, :])
    mixed_parts[:, :SLOTS] = high
    mixed_parts[:, SLOTS : 2 * SLOTS] = high
    mixed_parts[:, 2 * SLOTS :] = low

    tables[4].wait()
    spread_tiles = spread_out.reshape(CHUNKS, GROUPS, 128, 128)

    def deposit(chunk):
        first = pl.multiple_of(chunk * 128, 128)
        high, low = halves(dot(table[pl.ds(first, 128), :], weight_z[...]))
        for place, value in enumerate((high, low, high)):
            pull_parts[chunk, place * 128 : place * 128 + 128, :SLOTS] = value
        atoms = dot_nt(jnp.concatenate([high, low, high], axis=1), mixed_parts[...])
        for group in range(GROUPS):
            spread_tiles[chunk, group] = atoms[:, group * 128 : group * 128 + 128]

    deposit(0)

    tables[5].wait()
    for tile in range(3):
        lanes = slice(tile * 128, tile * 128 + 128)
        for group in range(GROUPS):
            for y in range(CY):
                charge[tile, group * 128 + y * 8 : group * 128 + y * 8 + 8, :] = background[
                    y, group * 8 : group * 8 + 8, lanes
                ]
            charge[tile, group * 128 + CY * 8 : group * 128 + 128, :] = jnp.zeros(
                (128 - CY * 8, 128), F32
            )
    for side, first in ((0, 0), (1, 2 * 128 + 6)):
        pltpu.make_async_copy(halo_in.at[side], halo_in.at[side], recv_halo.at[side]).wait()
        for place in range(2):
            rows = pl.ds(first + place, EY, 8)
            for tile in range(3):
                lanes = slice(tile * 128, tile * 128 + 128)
                charge[tile, rows, :] += halo_in[side, place * EY : place * EY + EY, lanes]
    for tile in range(3):
        high, low = halves(charge[tile])
        for place, value in enumerate((high, high, low)):
            charge_parts[:, place * N + tile * 128 : place * N + tile * 128 + 128] = value

    def post_lines(chunk):
        pltpu.make_async_copy(
            spread_out.at[chunk, :, row], spread_in.at[chunk, :, :, row], recv_one.at[chunk]
        ).start()

        @pl.loop(0, ROWS)
        def _(step):
            target = row_target(step)

            @pl.when(step != ROWS - 2)
            def _():
                pltpu.make_async_remote_copy(
                    spread_out.at[chunk, :, target],
                    spread_in.at[chunk, :, :, row],
                    send_one.at[chunk],
                    recv_one.at[chunk],
                    device_id=in_rows(target),
                    device_id_type=MESH,
                ).start()

    def lines_left(chunk):
        sizes = spread_out.at[chunk, :, 0 : ROWS - 1]
        pltpu.make_async_copy(sizes, sizes, send_one.at[chunk]).wait()

    def add_frozen(chunk):
        first = pl.multiple_of(chunk * 128, 128)
        waves = dot_nt(table[pl.ds(first, 128), :], charge_parts[...])
        for group in range(GROUPS):
            spread_tiles[chunk, group] += waves[:, group * 128 : group * 128 + 128]

    add_frozen(0)
    post_lines(0)

    @pl.loop(1, CHUNKS)
    def _(chunk):
        deposit(chunk)
        add_frozen(chunk)

    lines_left(0)
    post_lines(1)

    def wave_left(unit):
        @pl.when(lax.rem(5 * unit + 8 * core, RING) != ring)
        def _():
            pltpu.make_async_copy(wave_out.at[unit], wave_out.at[unit], send_two.at[unit]).wait()

    def cells_left(place, step):
        target = ring_target(step)
        sent = back_out.at[place, target]
        pltpu.make_async_copy(sent, sent, send_three.at[place, target]).wait()

    tables[6].wait()
    spread_got = spread_in.reshape(CHUNKS, GROUPS, 128, 128)

    @pl.loop(0, CHUNKS)
    def _(chunk):
        pltpu.make_async_copy(spread_in.at[chunk], spread_in.at[chunk], recv_one.at[chunk]).wait()
        for group in range(GROUPS):
            flipped = spread_got[chunk, group].T
            for quarter in range(4):
                items = [flipped[(quarter * 4 + j) * 8 : (quarter * 4 + j) * 8 + 8] for j in range(4)]
                for k, item in enumerate(exchange_blocks(items)):
                    lines[
                        k * CX + group * 8 : k * CX + group * 8 + 8,
                        quarter * 128 : quarter * 128 + 128,
                    ] = item
        high, low = halves(lines[...])
        waves = dot(jnp.concatenate([high, high, low], axis=1), ahead_y[...])
        for k in range(4):
            for tile in range(3):
                wave_out[chunk * 12 + k * 3 + tile] = waves[
                    k * CX : k * CX + CX, tile * 128 : tile * 128 + 128
                ]

        @pl.loop(1, RING + 1)
        def _(step):
            target = ring_target(step)
            within = lax.rem(13 * (target + RING - 8 * core) + RING * 12 - chunk * 12, RING)
            unit = chunk * 12 + within
            place = lax.div(unit, RING)

            @pl.when((chunk > 0) & (within < 12))
            def _():
                wave_left(unit - 12)

            @pl.when((target != ring) & (within < 12))
            def _():
                pltpu.make_async_remote_copy(
                    wave_out.at[unit],
                    wave_in.at[place, ring],
                    send_two.at[unit],
                    recv_two.at[place],
                    device_id=in_ring(target),
                    device_id_type=MESH,
                ).start()

            @pl.when((target == ring) & (within < 12))
            def _():
                pltpu.make_async_copy(
                    wave_out.at[unit], wave_in.at[place, ring], recv_two.at[place]
                ).start()

        @pl.when(chunk == 0)
        def _():
            lines_left(1)
            post_lines(2)

    slope_y = spline_slope(offset_y)
    slope_x = spline_slope(offset_x)
    fill_z(spline_slope, slope_z)
    high, low = halves(dot(table[...], slope_z[...]))
    for chunk in range(CHUNKS):
        for place, value in enumerate((high, low, high)):
            pull_parts[chunk, place * 128 : place * 128 + 128, SLOTS:] = value[
                chunk * 128 : chunk * 128 + 128
            ]

    for copy in tables[7:9]:
        copy.wait()
    base = lax.rem(13 * (ring + RING - 8 * core), RING)
    n_places = lax.div(UNITS - 1 - base, RING) + 1

    @pl.loop(0, n_places)
    def _(place):
        unit = place * RING + base
        pltpu.make_async_copy(
            wave_in.at[place, :], wave_in.at[place, :], recv_two.at[place]
        ).wait()
        high, low = halves(wave_in[place].reshape(N, 128))
        waves = dot(table[...], jnp.concatenate([high, high, low], axis=0))
        within = lax.rem(unit, 12)
        wave_z = lax.div(unit, 12) * 128 + row * 4 + lax.div(within, 3)
        tile = lax.rem(within, 3)
        decay = green_x[0, pl.ds(wave_z, 1), :] * green_y[0, tile]
        square = green_x[1, pl.ds(wave_z, 1), :] + green_y[1, tile]
        squares = green_x[1].reshape(N // 8, 8, 128) + square[None]
        decays = green_x[0].reshape(N // 8, 8, 128) * decay[None]
        green = jnp.where(squares > 0.0, decays / jnp.where(squares > 0.0, squares, 1.0), 0.0)
        high, low = halves(waves * green.reshape(N, 128))
        cells = dot(table[...], jnp.concatenate([high, high, low], axis=0))
        back_out[place] = cells.reshape(RING, CX, 128)
        group = lax.div(unit, 12)
        pltpu.make_async_copy(
            back_out.at[place, ring], back_in.at[unit], recv_three.at[group]
        ).start()

        @pl.loop(1, RING)
        def _(step):
            target = ring_target(step)

            @pl.when((place == 0) & (step <= 12))
            def _():
                wave_left(24 + lax.rem(step - 1 + lax.div(3 * ring, 4), 12))

            @pl.when(place > 0)
            def _():
                cells_left(place - 1, step)

            pltpu.make_async_remote_copy(
                back_out.at[place, target],
                back_in.at[unit],
                send_three.at[place, target],
                recv_three.at[group],
                device_id=in_ring(target),
                device_id_type=MESH,
            ).start()

    tables[9].wait()
    cell_tiles = cell_out.reshape(CHUNKS, GROUPS, 128, 128)

    @pl.loop(0, CHUNKS)
    def _(chunk):
        units = pl.ds(chunk * 12, 12)
        pltpu.make_async_copy(
            back_in.at[units], back_in.at[units], recv_three.at[chunk]
        ).wait()
        tiles = [
            jnp.concatenate([back_in[chunk * 12 + k * 3 + tile] for tile in range(3)], axis=1)
            for k in range(4)
        ]
        high, low = halves(jnp.concatenate(tiles, axis=0))
        lines[...] = dot(jnp.concatenate([high, high, low], axis=1), back_y[...])
        for group in range(GROUPS):
            for quarter in range(4):
                items = [
                    lines[
                        k * CX + group * 8 : k * CX + group * 8 + 8,
                        quarter * 128 : quarter * 128 + 128,
                    ]
                    for k in range(4)
                ]
                for j, item in enumerate(exchange_blocks(items)):
                    turned[(quarter * 4 + j) * 8 : (quarter * 4 + j) * 8 + 8, :] = item
            cell_tiles[chunk, group] = turned[...].T
        pltpu.make_async_copy(
            cell_out.at[chunk, :, :, row], cell_in.at[chunk, :, row], recv_four.at[chunk]
        ).start()

        @pl.loop(0, ROWS)
        def _(step):
            target = row_target(step)

            @pl.when(step != ROWS - 2)
            def _():
                pltpu.make_async_remote_copy(
                    cell_out.at[chunk, :, :, target],
                    cell_in.at[chunk, :, row],
                    send_four.at[chunk],
                    recv_four.at[chunk],
                    device_id=in_rows(target),
                    device_id_type=MESH,
                ).start()

    lines_left(2)
    for side in range(2):
        pltpu.make_async_copy(halo_out.at[side], halo_out.at[side], send_halo.at[side]).wait()

    @pl.loop(1, RING)
    def _(step):
        cells_left(n_places - 1, step)

    cell_got = cell_in.reshape(CHUNKS, GROUPS, 128, 128)
    gathered[...] = jnp.zeros((MAIN + EDGE, 2 * SLOTS), F32)

    @pl.loop(0, CHUNKS)
    def _(chunk):
        pltpu.make_async_copy(cell_in.at[chunk], cell_in.at[chunk], recv_four.at[chunk]).wait()
        for side, group, first in ((0, 2, 2 * 128 + 6), (1, 0, 0)):
            cells[group * 128 : group * 128 + 128, :] = cell_got[chunk, group].T
            for place in range(2):
                flank_out[chunk, side, place * EY : place * EY + EY, :] = cells[
                    pl.ds(first + place, EY, 8), :
                ]
            pltpu.make_async_remote_copy(
                flank_out.at[chunk, side],
                flank_in.at[chunk, side],
                send_flank.at[chunk, side],
                recv_flank.at[chunk, side],
                device_id=in_ring(sides[side]),
                device_id_type=MESH,
            ).start()
        cells[128:256, :] = cell_got[chunk, 1].T
        high, low = halves(cells[...])
        gathered[:MAIN, :] += dot(jnp.concatenate([high, high, low], axis=1), pull_parts[chunk])

    force_x = jnp.zeros((8, SLOTS), F32)
    force_y = jnp.zeros((8, SLOTS), F32)
    force_z = jnp.zeros((8, SLOTS), F32)
    for y in range(EY):
        along_x = jnp.zeros((8, SLOTS), F32)
        turned_x = jnp.zeros((8, SLOTS), F32)
        depth_x = jnp.zeros((8, SLOTS), F32)
        for group in range(GROUPS):
            first = group * 128 + y * 8
            plain = gathered[first : first + 8, :SLOTS]
            deriv = gathered[first : first + 8, SLOTS:]
            weight = height_x[group * 8 : group * 8 + 8]
            along_x += weight * plain
            turned_x += slope_x[group * 8 : group * 8 + 8] * plain
            depth_x += weight * deriv
        force_x += height_y[y : y + 1] * turned_x
        force_y += slope_y[y : y + 1] * along_x
        force_z += height_y[y : y + 1] * depth_x
    @pl.loop(0, CHUNKS)
    def _(chunk):
        for side in range(2):
            pltpu.make_async_copy(
                flank_in.at[chunk, side], flank_in.at[chunk, side], recv_flank.at[chunk, side]
            ).wait()
        high, low = halves(flank_in[chunk].reshape(EDGE, 128))
        gathered[MAIN:, :] += dot(jnp.concatenate([high, high, low], axis=1), pull_parts[chunk])

    for half in range(2):
        along_x = jnp.zeros((8, SLOTS), F32)
        turned_x = jnp.zeros((8, SLOTS), F32)
        depth_x = jnp.zeros((8, SLOTS), F32)
        for place, x in enumerate((CX + 2, CX + 3, CX, CX + 1)):
            first = MAIN + place * EY + half * 8
            plain = gathered[first : first + 8, :SLOTS]
            deriv = gathered[first : first + 8, SLOTS:]
            along_x += height_x[x : x + 1] * plain
            turned_x += slope_x[x : x + 1] * plain
            depth_x += height_x[x : x + 1] * deriv
        height = height_y[half * 8 : half * 8 + 8]
        force_x += height * turned_x
        force_y += slope_y[half * 8 : half * 8 + 8] * along_x
        force_z += height * depth_x
    for place, force in enumerate((force_x, force_y, force_z)):
        out[place, 0] = -live * jnp.sum(force, axis=0, keepdims=True)

    @pl.loop(0, CHUNKS)
    def _(chunk):
        sizes = cell_in.at[chunk, :, 0 : ROWS - 1]
        pltpu.make_async_copy(sizes, sizes, send_four.at[chunk]).wait()
        for side in range(2):
            sizes = flank_out.at[chunk, side]
            pltpu.make_async_copy(sizes, sizes, send_flank.at[chunk, side]).wait()


def solution(mesh):
    tables = make_tables()

    def per_device(*args):
        vmem = pl.BlockSpec(memory_space=pltpu.VMEM)
        anywhere = pl.BlockSpec(memory_space=pl.ANY)
        held = [pltpu.VMEM(value.shape, value.dtype) for value in (*args[:4], args[5], *tables)]
        return pl.pallas_call(
            kernel,
            out_shape=jax.ShapeDtypeStruct((3, 1, 1, SLOTS), F32),
            in_specs=[anywhere] * 4 + [pl.BlockSpec(memory_space=pltpu.SMEM)] + [anywhere] * 6,
            out_specs=vmem,
            scratch_shapes=held
            + [
                pltpu.SemaphoreType.DMA((10,)),
                pltpu.VMEM((3 * N, SLOTS), BF16),
                pltpu.VMEM((3 * N, SLOTS), BF16),
                pltpu.VMEM((MAIN + EDGE, SLOTS), F32),
                pltpu.VMEM((MAIN, 3 * SLOTS), BF16),
                pltpu.VMEM((3, MAIN, 128), F32),
                pltpu.VMEM((MAIN, 3 * N), BF16),
                pltpu.VMEM((CHUNKS, 3 * 128, 2 * SLOTS), BF16),
                pltpu.VMEM((4 * CX, EY * ROWS), F32),
                pltpu.VMEM((128, 128), F32),
                pltpu.VMEM((CHUNKS, GROUPS, ROWS, 4, 1, 128), F32),
                pltpu.VMEM((CHUNKS, GROUPS, 4, ROWS, 1, 128), F32),
                pltpu.VMEM((UNITS, CX, 128), F32),
                pltpu.VMEM((3, RING, CX, 128), F32),
                pltpu.VMEM((3, RING, CX, 128), F32),
                pltpu.VMEM((UNITS, CX, 128), F32),
                pltpu.VMEM((CHUNKS, GROUPS, 4, ROWS, 1, 128), F32),
                pltpu.VMEM((CHUNKS, GROUPS, ROWS, 4, 1, 128), F32),
                pltpu.VMEM((2, 32, N), F32),
                pltpu.VMEM((2, 32, N), F32),
                pltpu.VMEM((CHUNKS, 2, 32, 128), F32),
                pltpu.VMEM((CHUNKS, 2, 32, 128), F32),
                pltpu.VMEM((MAIN, 128), F32),
                pltpu.VMEM((MAIN + EDGE, 2 * SLOTS), F32),
                pltpu.SemaphoreType.DMA((CHUNKS,)),
                pltpu.SemaphoreType.DMA((CHUNKS,)),
                pltpu.SemaphoreType.DMA((UNITS,)),
                pltpu.SemaphoreType.DMA((3,)),
                pltpu.SemaphoreType.DMA((3, RING)),
                pltpu.SemaphoreType.DMA((CHUNKS,)),
                pltpu.SemaphoreType.DMA((CHUNKS,)),
                pltpu.SemaphoreType.DMA((CHUNKS,)),
                pltpu.SemaphoreType.DMA((2,)),
                pltpu.SemaphoreType.DMA((2,)),
                pltpu.SemaphoreType.DMA((CHUNKS, 2)),
                pltpu.SemaphoreType.DMA((CHUNKS, 2)),
            ],
            compiler_params=pltpu.CompilerParams(
                collective_id=0, has_side_effects=True, vmem_limit_bytes=60 * 1024 * 1024
            ),
            name="ewald",
        )(*args, *(jnp.asarray(table) for table in tables))

    pencils = P("gx", ("gy", "gz"), None)
    return jax.shard_map(
        per_device,
        mesh=mesh,
        in_specs=(pencils,) * 4 + (P("gx", ("gy", "gz")), P(("gy", "gz"), "gx", None)),
        out_specs=P(None, "gx", ("gy", "gz"), None),
        check_vma=False,
    )
```

```python
import math

import jax
import jax.numpy as jnp
import ml_dtypes
import numpy as np
from jax import lax
from jax.experimental import pallas as pl
from jax.experimental.pallas import tpu as pltpu
from jax.sharding import PartitionSpec as P

COULOMB = 6.5
N = 384
RING = 16
ROWS = 32
CX, CY = N // RING, N // ROWS
EY = 16
GROUPS = CX // 8
MAIN = GROUPS * 128
EDGE = 64
SLOTS = 256
CHUNKS = 3
UNITS = 36
MESH = pl.DeviceIdType.MESH
F32 = jnp.float32
BF16 = jnp.bfloat16


def parts(table):
    high = table.astype(ml_dtypes.bfloat16)
    low = (table - high.astype(np.float64)).astype(ml_dtypes.bfloat16)
    return high, low


def cas(rows, columns):
    angles = (rows[:, None] * columns[None, :] % N) * (2.0 * math.pi / N)
    return np.cos(angles) + np.sin(angles)


def wide_table(table):
    high, low = parts(table)
    return np.concatenate([high, low, high], axis=1)


def tall_table(table):
    high, low = parts(table)
    return np.concatenate([high, low, high], axis=0)


def make_tables():
    wave = np.arange(N)
    along = wide_table(cas(wave, wave))
    inner_y = np.arange(EY)
    inner_y = np.where(inner_y < CY + 2, inner_y, inner_y - EY)
    cell_y = (inner_y[:, None] + CY * np.arange(ROWS)[None, :]).reshape(-1) % N
    ahead_y = tall_table(cas(cell_y, wave))
    back_y = tall_table(cas(wave, cell_y))
    signed = np.where(wave <= N // 2, wave, wave - N) / N
    angles = 2.0 * math.pi / N * wave
    modulus = (230.0 + 152.0 * np.cos(angles) + 2.0 * np.cos(2.0 * angles)) / 384.0
    decay = np.exp(-(math.pi**2) * signed**2) / modulus**2
    factor = COULOMB / (math.pi * N * N * N)
    green_x = np.broadcast_to(np.stack([decay, signed**2])[:, :, None], (2, N, 128))
    green_y = np.stack([decay * factor, signed**2]).reshape(2, 3, 1, 128)
    green_y = np.broadcast_to(green_y, (2, 3, 8, 128))
    return (
        along,
        ahead_y,
        back_y,
        np.ascontiguousarray(green_x, dtype=np.float32),
        np.ascontiguousarray(green_y, dtype=np.float32),
    )


def ramps(offset):
    distance = jnp.minimum(offset, 5.0 - offset)
    return (
        jnp.maximum(distance, 0.0),
        jnp.maximum(distance - 1.0, 0.0),
        jnp.maximum(distance - 2.0, 0.0),
    )


def spline(offset):
    zero, one, two = (ramp * ramp for ramp in ramps(offset))
    return (zero * zero - 5.0 * (one * one) + 10.0 * (two * two)) * (1.0 / 24.0)


def spline_slope(offset):
    zero, one, two = (ramp * ramp * ramp for ramp in ramps(offset))
    slope = (zero - 5.0 * one + 10.0 * two) * (1.0 / 6.0)
    return jnp.where(offset < 2.5, slope, -slope)


def halves(value):
    high = value.astype(BF16)
    return high, (value - high.astype(F32)).astype(BF16)


def dot(left, right):
    return jnp.dot(left, right, preferred_element_type=F32)


def dot_nt(left, right):
    return lax.dot_general(left, right, (((1,), (1,)), ((), ())), preferred_element_type=F32)


def exchange_blocks(items):
    lane = lax.broadcasted_iota(jnp.int32, (8, 128), 1)
    low = lane < 64
    even = (lane // 32) % 2 == 0

    def pair(first, second, shift, mask):
        back = pltpu.roll(second, shift, 1)
        ahead = pltpu.roll(first, 128 - shift, 1)
        return jnp.where(mask, first, back), jnp.where(mask, ahead, second)

    zero, two = pair(items[0], items[2], 64, low)
    one, three = pair(items[1], items[3], 64, low)
    zero, one = pair(zero, one, 32, even)
    two, three = pair(two, three, 32, even)
    return zero, one, two, three


def kernel(
    atom_x_hbm,
    atom_y_hbm,
    atom_z_hbm,
    charges_hbm,
    counts,
    background_hbm,
    table_hbm,
    ahead_y_hbm,
    back_y_hbm,
    green_x_hbm,
    green_y_hbm,
    out,
    atom_x,
    atom_y,
    atom_z,
    charges,
    background,
    table,
    ahead_y,
    back_y,
    green_x,
    green_y,
    table_sem,
    weight_z,
    slope_z,
    mixed,
    mixed_parts,
    charge,
    charge_parts,
    pull_parts,
    lines,
    turned,
    spread_out,
    spread_in,
    wave_out,
    wave_in,
    back_out,
    back_in,
    cell_out,
    cell_in,
    halo_out,
    halo_in,
    flank_out,
    flank_in,
    cells,
    gathered,
    send_one,
    recv_one,
    send_two,
    recv_two,
    send_three,
    recv_three,
    send_four,
    recv_four,
    send_halo,
    recv_halo,
    send_flank,
    recv_flank,
):
    ring = lax.axis_index("gx")
    major, minor = lax.axis_index("gy"), lax.axis_index("gz")
    row = major * 4 + minor
    core = lax.rem(minor, 2)

    def in_ring(index):
        return (index, major, minor)

    def in_rows(index):
        return (ring, lax.div(index, 4), lax.rem(index, 4))

    tables = [
        pltpu.make_async_copy(source, target, table_sem.at[place])
        for place, (source, target) in enumerate(
            (
                (atom_x_hbm, atom_x),
                (atom_y_hbm, atom_y),
                (atom_z_hbm, atom_z),
                (charges_hbm, charges),
                (table_hbm, table),
                (background_hbm, background),
                (ahead_y_hbm, ahead_y),
                (green_x_hbm, green_x),
                (green_y_hbm, green_y),
                (back_y_hbm, back_y),
            )
        )
    ]
    for copy in tables[:5]:
        copy.start()

    barrier = pltpu.get_barrier_semaphore()

    def far_first(step, size):
        half = lax.div(step, 2)
        return size // 2 + jnp.where(lax.rem(step, 2) == 1, half, -half)

    def ring_target(step):
        return lax.rem(ring + far_first(step, RING), RING)

    chip_x = 2 * lax.div(minor, 2) + lax.div(major, 4)
    chip_y = lax.rem(major, 4)

    def row_target(step):
        x = lax.rem(chip_x + far_first(lax.div(step, 8) + 1, 4), 4)
        y = lax.rem(chip_y + far_first(lax.rem(lax.div(step, 2), 4) + 1, 4), 4)
        other = lax.rem(core + step, 2)
        return (4 * lax.rem(x, 2) + y) * 4 + 2 * lax.div(x, 2) + other

    for step in range(1, RING):
        pl.semaphore_signal(
            barrier, inc=1, device_id=in_ring(ring_target(step)), device_id_type=MESH
        )
    for step in range(ROWS):
        if step != ROWS - 2:
            pl.semaphore_signal(
                barrier, inc=1, device_id=in_rows(row_target(step)), device_id_type=MESH
            )

    for copy in tables[5:]:
        copy.start()

    for copy in tables[:4]:
        copy.wait()
    slot = lax.broadcasted_iota(jnp.int32, (1, SLOTS), 1)
    live = jnp.where(slot < counts[0, 0], charges[0], 0.0)
    inner_y = lax.broadcasted_iota(jnp.int32, (EY, SLOTS), 0)
    inner_y = jnp.where(inner_y < CY + 2, inner_y, inner_y - EY).astype(F32)
    offset_y = atom_y[0] - inner_y + 2.5
    height_y = spline(offset_y)
    inner_x = lax.broadcasted_iota(jnp.int32, (CX + 8, SLOTS), 0)
    inner_x = jnp.where(inner_x < CX + 2, inner_x, inner_x - CX - 4).astype(F32)
    offset_x = atom_x[0] - inner_x + 2.5
    height_x = spline(offset_x)

    def fill_z(function, target):
        @pl.loop(0, N // 64)
        def _(block):
            first = pl.multiple_of(block * 64, 64)
            plane = (lax.broadcasted_iota(jnp.int32, (64, SLOTS), 0) + first).astype(F32)
            offset = atom_z[0] - plane
            offset = jnp.where(offset >= N / 2.0, offset - N, offset)
            offset = jnp.where(offset < -N / 2.0, offset + N, offset)
            high, low = halves(function(offset + 2.5))
            target[pl.ds(first, 64), :] = high
            target[pl.ds(N + first, 64), :] = high
            target[pl.ds(2 * N + first, 64), :] = low

    fill_z(spline, weight_z)
    charged_y = height_y * live
    for place in range(4):
        mixed[MAIN + place * EY : MAIN + place * EY + EY, :] = (
            height_x[CX + place : CX + place + 1] * charged_y
        )
    high, low = halves(mixed[MAIN:, :])
    edges = (
        dot_nt(high, weight_z[:N, :])
        + dot_nt(high, weight_z[2 * N :, :])
        + dot_nt(low, weight_z[:N, :])
    )
    for side in range(2):
        halo_out[side] = edges[side * 32 : side * 32 + 32]

    pl.semaphore_wait(barrier, ROWS - 1 + RING - 1)
    sides = (lax.rem(ring + 1, RING), lax.rem(ring + RING - 1, RING))
    for side in range(2):
        pltpu.make_async_remote_copy(
            halo_out.at[side],
            halo_in.at[side],
            send_halo.at[side],
            recv_halo.at[side],
            device_id=in_ring(sides[side]),
            device_id_type=MESH,
        ).start()

    for y in range(EY):
        for group in range(GROUPS):
            mixed[group * 128 + y * 8 : group * 128 + y * 8 + 8, :] = (
                height_x[group * 8 : group * 8 + 8] * charged_y[y : y + 1]
            )
    high, low = halves(mixed[:MAIN, :])
    mixed_parts[:, :SLOTS] = high
    mixed_parts[:, SLOTS : 2 * SLOTS] = high
    mixed_parts[:, 2 * SLOTS :] = low

    tables[4].wait()
    spread_tiles = spread_out.reshape(CHUNKS, GROUPS, 128, 128)

    def deposit(chunk):
        first = pl.multiple_of(chunk * 128, 128)
        high, low = halves(dot(table[pl.ds(first, 128), :], weight_z[...]))
        for place, value in enumerate((high, low, high)):
            pull_parts[chunk, place * 128 : place * 128 + 128, :SLOTS] = value
        atoms = dot_nt(jnp.concatenate([high, low, high], axis=1), mixed_parts[...])
        for group in range(GROUPS):
            spread_tiles[chunk, group] = atoms[:, group * 128 : group * 128 + 128]

    deposit(0)

    tables[5].wait()
    for tile in range(3):
        lanes = slice(tile * 128, tile * 128 + 128)
        for group in range(GROUPS):
            for y in range(CY):
                charge[tile, group * 128 + y * 8 : group * 128 + y * 8 + 8, :] = background[
                    y, group * 8 : group * 8 + 8, lanes
                ]
            charge[tile, group * 128 + CY * 8 : group * 128 + 128, :] = jnp.zeros(
                (128 - CY * 8, 128), F32
            )
    for side, first in ((0, 0), (1, 2 * 128 + 6)):
        pltpu.make_async_copy(halo_in.at[side], halo_in.at[side], recv_halo.at[side]).wait()
        for place in range(2):
            rows = pl.ds(first + place, EY, 8)
            for tile in range(3):
                lanes = slice(tile * 128, tile * 128 + 128)
                charge[tile, rows, :] += halo_in[side, place * EY : place * EY + EY, lanes]
    for tile in range(3):
        high, low = halves(charge[tile])
        for place, value in enumerate((high, high, low)):
            charge_parts[:, place * N + tile * 128 : place * N + tile * 128 + 128] = value

    def post_lines(chunk):
        pltpu.make_async_copy(
            spread_out.at[chunk, :, row], spread_in.at[chunk, :, :, row], recv_one.at[chunk]
        ).start()

        @pl.loop(0, ROWS)
        def _(step):
            target = row_target(step)

            @pl.when(step != ROWS - 2)
            def _():
                pltpu.make_async_remote_copy(
                    spread_out.at[chunk, :, target],
                    spread_in.at[chunk, :, :, row],
                    send_one.at[chunk],
                    recv_one.at[chunk],
                    device_id=in_rows(target),
                    device_id_type=MESH,
                ).start()

    def lines_left(chunk):
        sizes = spread_out.at[chunk, :, 0 : ROWS - 1]
        pltpu.make_async_copy(sizes, sizes, send_one.at[chunk]).wait()

    def add_frozen(chunk):
        first = pl.multiple_of(chunk * 128, 128)
        waves = dot_nt(table[pl.ds(first, 128), :], charge_parts[...])
        for group in range(GROUPS):
            spread_tiles[chunk, group] += waves[:, group * 128 : group * 128 + 128]

    add_frozen(0)
    post_lines(0)

    @pl.loop(1, CHUNKS)
    def _(chunk):
        deposit(chunk)
        add_frozen(chunk)

    lines_left(0)
    post_lines(1)

    def wave_left(unit):
        @pl.when(lax.rem(5 * unit + 8 * core, RING) != ring)
        def _():
            pltpu.make_async_copy(wave_out.at[unit], wave_out.at[unit], send_two.at[unit]).wait()

    def cells_left(place, step):
        target = ring_target(step)
        sent = back_out.at[place, target]
        pltpu.make_async_copy(sent, sent, send_three.at[place, target]).wait()

    tables[6].wait()
    spread_got = spread_in.reshape(CHUNKS, GROUPS, 128, 128)

    @pl.loop(0, CHUNKS)
    def _(chunk):
        pltpu.make_async_copy(spread_in.at[chunk], spread_in.at[chunk], recv_one.at[chunk]).wait()
        for group in range(GROUPS):
            flipped = spread_got[chunk, group].T
            for quarter in range(4):
                items = [flipped[(quarter * 4 + j) * 8 : (quarter * 4 + j) * 8 + 8] for j in range(4)]
                for k, item in enumerate(exchange_blocks(items)):
                    lines[
                        k * CX + group * 8 : k * CX + group * 8 + 8,
                        quarter * 128 : quarter * 128 + 128,
                    ] = item
        high, low = halves(lines[...])
        waves = dot(jnp.concatenate([high, high, low], axis=1), ahead_y[...])
        for k in range(4):
            for tile in range(3):
                wave_out[chunk * 12 + k * 3 + tile] = waves[
                    k * CX : k * CX + CX, tile * 128 : tile * 128 + 128
                ]

        @pl.loop(1, RING + 1, unroll=4)
        def _(step):
            target = ring_target(step)
            within = lax.rem(13 * (target + RING - 8 * core) + RING * 12 - chunk * 12, RING)
            unit = chunk * 12 + within
            place = lax.div(unit, RING)

            @pl.when((chunk > 0) & (within < 12))
            def _():
                wave_left(unit - 12)

            @pl.when((target != ring) & (within < 12))
            def _():
                pltpu.make_async_remote_copy(
                    wave_out.at[unit],
                    wave_in.at[place, ring],
                    send_two.at[unit],
                    recv_two.at[place],
                    device_id=in_ring(target),
                    device_id_type=MESH,
                ).start()

            @pl.when((target == ring) & (within < 12))
            def _():
                pltpu.make_async_copy(
                    wave_out.at[unit], wave_in.at[place, ring], recv_two.at[place]
                ).start()

        @pl.when(chunk == 0)
        def _():
            lines_left(1)
            post_lines(2)

    slope_y = spline_slope(offset_y)
    slope_x = spline_slope(offset_x)
    fill_z(spline_slope, slope_z)
    high, low = halves(dot(table[...], slope_z[...]))
    for chunk in range(CHUNKS):
        for place, value in enumerate((high, low, high)):
            pull_parts[chunk, place * 128 : place * 128 + 128, SLOTS:] = value[
                chunk * 128 : chunk * 128 + 128
            ]

    for copy in tables[7:9]:
        copy.wait()
    base = lax.rem(13 * (ring + RING - 8 * core), RING)
    n_places = lax.div(UNITS - 1 - base, RING) + 1

    @pl.loop(0, n_places)
    def _(place):
        unit = place * RING + base
        pltpu.make_async_copy(
            wave_in.at[place, :], wave_in.at[place, :], recv_two.at[place]
        ).wait()
        high, low = halves(wave_in[place].reshape(N, 128))
        waves = dot(table[...], jnp.concatenate([high, high, low], axis=0))
        within = lax.rem(unit, 12)
        wave_z = lax.div(unit, 12) * 128 + row * 4 + lax.div(within, 3)
        tile = lax.rem(within, 3)
        decay = green_x[0, pl.ds(wave_z, 1), :] * green_y[0, tile]
        square = green_x[1, pl.ds(wave_z, 1), :] + green_y[1, tile]
        squares = green_x[1].reshape(N // 8, 8, 128) + square[None]
        decays = green_x[0].reshape(N // 8, 8, 128) * decay[None]
        green = jnp.where(squares > 0.0, decays / jnp.where(squares > 0.0, squares, 1.0), 0.0)
        high, low = halves(waves * green.reshape(N, 128))
        cells = dot(table[...], jnp.concatenate([high, high, low], axis=0))
        back_out[place] = cells.reshape(RING, CX, 128)
        group = lax.div(unit, 12)
        pltpu.make_async_copy(
            back_out.at[place, ring], back_in.at[unit], recv_three.at[group]
        ).start()

        @pl.loop(1, RING, unroll=5)
        def _(step):
            target = ring_target(step)

            @pl.when((place == 0) & (step <= 12))
            def _():
                wave_left(24 + lax.rem(step - 1 + lax.div(3 * ring, 4), 12))

            @pl.when(place > 0)
            def _():
                cells_left(place - 1, step)

            pltpu.make_async_remote_copy(
                back_out.at[place, target],
                back_in.at[unit],
                send_three.at[place, target],
                recv_three.at[group],
                device_id=in_ring(target),
                device_id_type=MESH,
            ).start()

    tables[9].wait()
    cell_tiles = cell_out.reshape(CHUNKS, GROUPS, 128, 128)

    @pl.loop(0, CHUNKS)
    def _(chunk):
        units = pl.ds(chunk * 12, 12)
        pltpu.make_async_copy(
            back_in.at[units], back_in.at[units], recv_three.at[chunk]
        ).wait()
        tiles = [
            jnp.concatenate([back_in[chunk * 12 + k * 3 + tile] for tile in range(3)], axis=1)
            for k in range(4)
        ]
        high, low = halves(jnp.concatenate(tiles, axis=0))
        lines[...] = dot(jnp.concatenate([high, high, low], axis=1), back_y[...])
        for group in range(GROUPS):
            for quarter in range(4):
                items = [
                    lines[
                        k * CX + group * 8 : k * CX + group * 8 + 8,
                        quarter * 128 : quarter * 128 + 128,
                    ]
                    for k in range(4)
                ]
                for j, item in enumerate(exchange_blocks(items)):
                    turned[(quarter * 4 + j) * 8 : (quarter * 4 + j) * 8 + 8, :] = item
            cell_tiles[chunk, group] = turned[...].T
        pltpu.make_async_copy(
            cell_out.at[chunk, :, :, row], cell_in.at[chunk, :, row], recv_four.at[chunk]
        ).start()

        @pl.loop(0, ROWS)
        def _(step):
            target = row_target(step)

            @pl.when(step != ROWS - 2)
            def _():
                pltpu.make_async_remote_copy(
                    cell_out.at[chunk, :, :, target],
                    cell_in.at[chunk, :, row],
                    send_four.at[chunk],
                    recv_four.at[chunk],
                    device_id=in_rows(target),
                    device_id_type=MESH,
                ).start()

    lines_left(2)
    for side in range(2):
        pltpu.make_async_copy(halo_out.at[side], halo_out.at[side], send_halo.at[side]).wait()

    @pl.loop(1, RING)
    def _(step):
        cells_left(n_places - 1, step)

    cell_got = cell_in.reshape(CHUNKS, GROUPS, 128, 128)
    gathered[...] = jnp.zeros((MAIN + EDGE, 2 * SLOTS), F32)

    @pl.loop(0, CHUNKS)
    def _(chunk):
        pltpu.make_async_copy(cell_in.at[chunk], cell_in.at[chunk], recv_four.at[chunk]).wait()
        for side, group, first in ((0, 2, 2 * 128 + 6), (1, 0, 0)):
            cells[group * 128 : group * 128 + 128, :] = cell_got[chunk, group].T
            for place in range(2):
                flank_out[chunk, side, place * EY : place * EY + EY, :] = cells[
                    pl.ds(first + place, EY, 8), :
                ]
            pltpu.make_async_remote_copy(
                flank_out.at[chunk, side],
                flank_in.at[chunk, side],
                send_flank.at[chunk, side],
                recv_flank.at[chunk, side],
                device_id=in_ring(sides[side]),
                device_id_type=MESH,
            ).start()
        cells[128:256, :] = cell_got[chunk, 1].T
        high, low = halves(cells[...])
        gathered[:MAIN, :] += dot(jnp.concatenate([high, high, low], axis=1), pull_parts[chunk])

    force_x = jnp.zeros((8, SLOTS), F32)
    force_y = jnp.zeros((8, SLOTS), F32)
    force_z = jnp.zeros((8, SLOTS), F32)
    for y in range(EY):
        along_x = jnp.zeros((8, SLOTS), F32)
        turned_x = jnp.zeros((8, SLOTS), F32)
        depth_x = jnp.zeros((8, SLOTS), F32)
        for group in range(GROUPS):
            first = group * 128 + y * 8
            plain = gathered[first : first + 8, :SLOTS]
            deriv = gathered[first : first + 8, SLOTS:]
            weight = height_x[group * 8 : group * 8 + 8]
            along_x += weight * plain
            turned_x += slope_x[group * 8 : group * 8 + 8] * plain
            depth_x += weight * deriv
        force_x += height_y[y : y + 1] * turned_x
        force_y += slope_y[y : y + 1] * along_x
        force_z += height_y[y : y + 1] * depth_x
    @pl.loop(0, CHUNKS)
    def _(chunk):
        for side in range(2):
            pltpu.make_async_copy(
                flank_in.at[chunk, side], flank_in.at[chunk, side], recv_flank.at[chunk, side]
            ).wait()
        high, low = halves(flank_in[chunk].reshape(EDGE, 128))
        gathered[MAIN:, :] += dot(jnp.concatenate([high, high, low], axis=1), pull_parts[chunk])

    for half in range(2):
        along_x = jnp.zeros((8, SLOTS), F32)
        turned_x = jnp.zeros((8, SLOTS), F32)
        depth_x = jnp.zeros((8, SLOTS), F32)
        for place, x in enumerate((CX + 2, CX + 3, CX, CX + 1)):
            first = MAIN + place * EY + half * 8
            plain = gathered[first : first + 8, :SLOTS]
            deriv = gathered[first : first + 8, SLOTS:]
            along_x += height_x[x : x + 1] * plain
            turned_x += slope_x[x : x + 1] * plain
            depth_x += height_x[x : x + 1] * deriv
        height = height_y[half * 8 : half * 8 + 8]
        force_x += height * turned_x
        force_y += slope_y[half * 8 : half * 8 + 8] * along_x
        force_z += height * depth_x
    for place, force in enumerate((force_x, force_y, force_z)):
        out[place, 0] = -live * jnp.sum(force, axis=0, keepdims=True)

    @pl.loop(0, CHUNKS)
    def _(chunk):
        sizes = cell_in.at[chunk, :, 0 : ROWS - 1]
        pltpu.make_async_copy(sizes, sizes, send_four.at[chunk]).wait()
        for side in range(2):
            sizes = flank_out.at[chunk, side]
            pltpu.make_async_copy(sizes, sizes, send_flank.at[chunk, side]).wait()


def solution(mesh):
    tables = make_tables()

    def per_device(*args):
        vmem = pl.BlockSpec(memory_space=pltpu.VMEM)
        anywhere = pl.BlockSpec(memory_space=pl.ANY)
        held = [pltpu.VMEM(value.shape, value.dtype) for value in (*args[:4], args[5], *tables)]
        return pl.pallas_call(
            kernel,
            out_shape=jax.ShapeDtypeStruct((3, 1, 1, SLOTS), F32),
            in_specs=[anywhere] * 4 + [pl.BlockSpec(memory_space=pltpu.SMEM)] + [anywhere] * 6,
            out_specs=vmem,
            scratch_shapes=held
            + [
                pltpu.SemaphoreType.DMA((10,)),
                pltpu.VMEM((3 * N, SLOTS), BF16),
                pltpu.VMEM((3 * N, SLOTS), BF16),
                pltpu.VMEM((MAIN + EDGE, SLOTS), F32),
                pltpu.VMEM((MAIN, 3 * SLOTS), BF16),
                pltpu.VMEM((3, MAIN, 128), F32),
                pltpu.VMEM((MAIN, 3 * N), BF16),
                pltpu.VMEM((CHUNKS, 3 * 128, 2 * SLOTS), BF16),
                pltpu.VMEM((4 * CX, EY * ROWS), F32),
                pltpu.VMEM((128, 128), F32),
                pltpu.VMEM((CHUNKS, GROUPS, ROWS, 4, 1, 128), F32),
                pltpu.VMEM((CHUNKS, GROUPS, 4, ROWS, 1, 128), F32),
                pltpu.VMEM((UNITS, CX, 128), F32),
                pltpu.VMEM((3, RING, CX, 128), F32),
                pltpu.VMEM((3, RING, CX, 128), F32),
                pltpu.VMEM((UNITS, CX, 128), F32),
                pltpu.VMEM((CHUNKS, GROUPS, 4, ROWS, 1, 128), F32),
                pltpu.VMEM((CHUNKS, GROUPS, ROWS, 4, 1, 128), F32),
                pltpu.VMEM((2, 32, N), F32),
                pltpu.VMEM((2, 32, N), F32),
                pltpu.VMEM((CHUNKS, 2, 32, 128), F32),
                pltpu.VMEM((CHUNKS, 2, 32, 128), F32),
                pltpu.VMEM((MAIN, 128), F32),
                pltpu.VMEM((MAIN + EDGE, 2 * SLOTS), F32),
                pltpu.SemaphoreType.DMA((CHUNKS,)),
                pltpu.SemaphoreType.DMA((CHUNKS,)),
                pltpu.SemaphoreType.DMA((UNITS,)),
                pltpu.SemaphoreType.DMA((3,)),
                pltpu.SemaphoreType.DMA((3, RING)),
                pltpu.SemaphoreType.DMA((CHUNKS,)),
                pltpu.SemaphoreType.DMA((CHUNKS,)),
                pltpu.SemaphoreType.DMA((CHUNKS,)),
                pltpu.SemaphoreType.DMA((2,)),
                pltpu.SemaphoreType.DMA((2,)),
                pltpu.SemaphoreType.DMA((CHUNKS, 2)),
                pltpu.SemaphoreType.DMA((CHUNKS, 2)),
            ],
            compiler_params=pltpu.CompilerParams(
                collective_id=0, has_side_effects=True, vmem_limit_bytes=60 * 1024 * 1024
            ),
            name="ewald",
        )(*args, *(jnp.asarray(table) for table in tables))

    pencils = P("gx", ("gy", "gz"), None)
    return jax.shard_map(
        per_device,
        mesh=mesh,
        in_specs=(pencils,) * 4 + (P("gx", ("gy", "gz")), P(("gy", "gz"), "gx", None)),
        out_specs=P(None, "gx", ("gy", "gz"), None),
        check_vma=False,
    )
```
